256 devices in a mesh: lat: 16 (over y_lo, x, core), lon: 16 (over y_hi, z).
Axes of the slice: x: 4, y: 4 (y_hi: 2, y_lo: 2; y = y_hi * 2 + y_lo), z: 8, core: 2. Of those that a mesh axis runs over, the one named last changes fastest.
Arguments:
- features: bfloat16 [256, 256, 1024], P('lat', 'lon'), may hold values from -28 to 28
- w_qkv: bfloat16 [1024, 3072], replicated, may hold values from -0.078125 to 0.078125
- cotangent: bfloat16 [256, 256, 1024], P('lat', 'lon'), may hold values from -6 to 6
- row_reach: int32 [256], replicated, may hold values from 1 to 4, as said below
- col_reach: int32 [256], replicated, may hold values from 1 to 8, as said below
Outputs:
- attended: bfloat16 [256, 256, 1024], P('lat', 'lon')
- feature_grad: bfloat16 [256, 256, 1024], P('lat', 'lon')
The draws below stay inside these ranges and needn't reach their ends.
Inputs may be any that keep to these rules, and one draw needn't show every extreme that they name: `row_reach`: equal to 4 in the first and last rows. `col_reach`: equal to 8 in the first and last rows.
All inputs are finite; a program needn't handle non-finite values.
Results may differ from the reference program's by a relative error of at most 0.012.
The reference program's roundings to bfloat16 on the way (of `qkv`, `prob_b`, `d_score` and `d_qkv`) count: a program that leaves them out, or rounds other values in their place, can miss the bound.
Values may be sent and summed in bfloat16 or wider, within the bound.
A program may use at most 128 MiB of HBM per device.

```python
import math
import jax
import jax.numpy as jnp
from jax import lax

CHANNELS = 1024
HEADS = 16
RMAX = 4
CMAX = 8
LAT_ROWS = 256
LON_COLS = 256


def reach_table(key, largest):
    row_index = jnp.arange(LAT_ROWS, dtype=jnp.int32)
    pole_dist = jnp.minimum(row_index, LAT_ROWS - 1 - row_index)
    widening = largest - 2 * pole_dist * largest // LAT_ROWS
    jitter_step = jax.random.randint(key, (LAT_ROWS,), 0, 2) * (pole_dist > 0).astype(jnp.int32)
    return jnp.clip(widening - jitter_step, 1, largest).astype(jnp.int32)


def draw_row_reach(key, part):
    return reach_table(jax.random.fold_in(key, 11), RMAX)


def draw_col_reach(key, part):
    return reach_table(jax.random.fold_in(key, 23), CMAX)


def draw_features(key, part):
    base_key = jax.random.fold_in(jax.random.fold_in(key, 31), 0)
    grid_shape = (LAT_ROWS, LON_COLS, CHANNELS)
    base_field = jax.random.normal(base_key, grid_shape, jnp.float32)
    return jnp.clip(base_field, -6.0, 6.0).astype(jnp.bfloat16)


def draw_w_qkv(key, part):
    first_key, second_key, third_key = jax.random.split(jax.random.fold_in(key, 47), 3)
    square = (CHANNELS, CHANNELS)
    fan_scale = CHANNELS ** (-0.5)
    query_part = jnp.clip(jax.random.normal(first_key, square, jnp.float32), -2.5, 2.5)
    key_part = jnp.clip(jax.random.normal(second_key, square, jnp.float32), -2.5, 2.5)
    value_part = jnp.clip(jax.random.normal(third_key, square, jnp.float32), -2.5, 2.5)
    joined = jnp.concatenate([query_part, key_part, value_part], 1) * fan_scale
    return joined.astype(jnp.bfloat16)


def level_of(rng, shape, cuts, least, high):
    loudness = 1.0
    for dim, blocks in cuts:
        draws = jax.random.uniform(jax.random.fold_in(jax.random.fold_in(rng, 6), dim), (blocks,), jnp.float32, least / len(cuts), high / len(cuts))
        loudness = loudness * jnp.repeat(jnp.exp(draws), shape[dim] // blocks).reshape((-1,) + (1,) * (len(shape) - 1 - dim))
    return loudness


def bell_draw(own_key, shape, scale, bound, pieces=(), held_as=jnp.bfloat16):
    entries = jax.random.normal(own_key, shape, jnp.float32) * scale
    if len(pieces) > 0:
        entries = level_of(own_key, shape, pieces, -0.22, 0.18) * entries
    return jnp.clip(entries, min=-bound, max=bound).astype(held_as)


def setup_inputs(seed: int = 0) -> dict:
    splits = jax.random.split(jax.random.key(seed), 6)
    features = draw_features(jax.random.fold_in(splits[5], 71), 0)
    w_qkv = draw_w_qkv(jax.random.fold_in(splits[5], 71), 0)
    cotangent = bell_draw(splits[2], (LAT_ROWS, LON_COLS, CHANNELS), 1.0, 6.0, ((0, 16), (1, 16)))
    row_reach = draw_row_reach(jax.random.fold_in(splits[5], 71), 0)
    col_reach = draw_col_reach(jax.random.fold_in(splits[5], 71), 0)
    return {"features": features, "w_qkv": w_qkv, "cotangent": cotangent, "row_reach": row_reach, "col_reach": col_reach}


def to_half(values):
    return lax.optimization_barrier(values.astype(jnp.bfloat16)).astype(jnp.float32)

def reference(features, w_qkv, cotangent, row_reach, col_reach):
    height, width, n_chan = features.shape
    head_dim = n_chan // HEADS
    scale = 1.0 / math.sqrt(head_dim)
    qkv = jnp.dot(features.reshape(-1, n_chan), w_qkv, preferred_element_type=jnp.float32)
    qkv = qkv.astype(jnp.bfloat16).reshape(height, width, 3 * n_chan)
    query = qkv[..., :n_chan]
    padding = ((RMAX, RMAX), (0, 0), (0, 0))
    key_pad = jnp.pad(qkv[..., n_chan:2 * n_chan], padding)
    val_pad = jnp.pad(qkv[..., 2 * n_chan:], padding)
    row_off = jnp.arange(2 * RMAX + 1, dtype=jnp.int32) - RMAX
    col_off = jnp.arange(2 * CMAX + 1, dtype=jnp.int32) - CMAX
    n_off = (2 * RMAX + 1) * (2 * CMAX + 1)

    def window(block):
        parts = [jnp.roll(block, -shift, axis=1) for shift in range(-CMAX, CMAX + 1)]
        stacked = jnp.stack(parts, axis=1).reshape(n_off, width, HEADS, head_dim)
        return stacked.astype(jnp.float32)

    def one_row(carry, inputs):
        row, q_row, g_row = inputs
        k_win = window(lax.dynamic_slice_in_dim(key_pad, row, 2 * RMAX + 1, 0))
        v_win = window(lax.dynamic_slice_in_dim(val_pad, row, 2 * RMAX + 1, 0))
        key_row = row + row_off
        ok_row = (jnp.abs(row_off) <= row_reach[row]) & (key_row >= 0) & (key_row < height)
        ok_col = jnp.abs(col_off) <= col_reach[row]
        usable = (ok_row[:, None] & ok_col[None, :]).reshape(-1)
        q_val = q_row.astype(jnp.float32).reshape(width, HEADS, head_dim)
        g_val = g_row.astype(jnp.float32).reshape(width, HEADS, head_dim)
        scores = jnp.einsum('whe,owhe->who', q_val, k_win) * scale
        scores = jnp.where(usable, scores, -1e+30)
        peak = lax.optimization_barrier(jnp.max(scores, axis=-1, keepdims=True))
        expo = jnp.exp(scores - peak)
        prob = expo / lax.optimization_barrier(jnp.sum(expo, axis=-1, keepdims=True))
        prob_b = to_half(prob)
        outrow = jnp.einsum('who,owhe->whe', prob_b, v_win)
        d_prob = jnp.einsum('whe,owhe->who', g_val, v_win)
        delta = lax.optimization_barrier(jnp.sum(prob * d_prob, axis=-1, keepdims=True))
        d_score = to_half(prob * (d_prob - delta) * scale)
        d_query = jnp.einsum('who,owhe->whe', d_score, k_win)
        d_key = jnp.einsum('who,whe->owhe', d_score, q_val)
        d_value = jnp.einsum('who,whe->owhe', prob_b, g_val)
        grads = jnp.concatenate([d_key.reshape(n_off, width, n_chan), d_value.reshape(n_off, width, n_chan)], -1)
        grads = grads.reshape(2 * RMAX + 1, 2 * CMAX + 1, width, 2 * n_chan)
        back = jnp.zeros((2 * RMAX + 1, width, 2 * n_chan), jnp.float32)
        for index in range(2 * CMAX + 1):
            back = back + jnp.roll(grads[:, index], index - CMAX, axis=1)
        update = lax.dynamic_slice_in_dim(carry, row, 2 * RMAX + 1, 0) + back
        carry = lax.dynamic_update_slice_in_dim(carry, update, row, 0)
        return (carry, (outrow.reshape(width, n_chan).astype(jnp.bfloat16), d_query.reshape(width, n_chan)))
    start = jnp.zeros((height + 2 * RMAX, width, 2 * n_chan), jnp.float32)
    rows_all = jnp.arange(height, dtype=jnp.int32)
    carry, (attended, d_query) = lax.scan(one_row, start, (rows_all, query, cotangent))
    own = carry[RMAX:RMAX + height]
    d_qkv = jnp.concatenate([d_query, own], -1).astype(jnp.bfloat16).reshape(-1, 3 * n_chan)
    feature_grad = jnp.dot(d_qkv, w_qkv.T, preferred_element_type=jnp.float32)
    feature_grad = feature_grad.astype(jnp.bfloat16).reshape(height, width, n_chan)
    return (attended, feature_grad)
```

```python
import jax
import jax.numpy as jnp
from jax import lax
from jax.experimental import pallas as pl
from jax.experimental.pallas import tpu as pltpu
from jax.sharding import PartitionSpec as P

HEADS = 16
RMAX = 4
CMAX = 8
CHAN = 1024
GROUP = 256
NGROUP = CHAN // GROUP
F32 = jnp.float32
BF16 = jnp.bfloat16
MESH = pl.DeviceIdType.MESH
NN = (((1,), (0,)), ((), ()))
NT = (((1,), (1,)), ((), ()))
TN = (((0,), (0,)), ((), ()))


def dot(a, b, dims):
    return lax.dot_general(a, b, dims, preferred_element_type=F32)


def block_diagonal(x):
    rows = lax.broadcasted_iota(jnp.int32, (256, GROUP), 0) // 64
    cols = lax.broadcasted_iota(jnp.int32, (256, GROUP), 1) // 64
    return jnp.where(rows == cols, jnp.concatenate([x] * 4, 0), jnp.zeros((), x.dtype))


def take_diagonal(o):
    cols = lax.broadcasted_iota(jnp.int32, (64, GROUP), 1) // 64
    out = o[:64]
    for head in range(1, 4):
        out = jnp.where(cols == head, o[64 * head : 64 * head + 64], out)
    return out


def kernel(
    x_hbm, w_hbm, g_ref, rr_ref, cc_ref, att_ref, fg_ref,
    xm, xl, xr, edge_l, edge_r, w, q, k, v, dk, dv, dq, bias, grads,
    tb_send, tb_recv, side_send, side_recv,
    local_sem, send_sem, recv_sem,
):
    lat, lon = lax.axis_index("lat"), lax.axis_index("lon")
    n_lat, n_lon = lax.axis_size("lat"), lax.axis_size("lon")
    up = (lax.rem(lat + n_lat - 1, n_lat), lon)
    down = (lax.rem(lat + 1, n_lat), lon)
    left = (lat, lax.rem(lon + n_lon - 1, n_lon))
    right = (lat, lax.rem(lon + 1, n_lon))

    own_copy = pltpu.make_async_copy(x_hbm, xm.at[4:20], local_sem.at[0])
    own_copy.start()
    w_copies = []
    for part in range(3):
        cols = slice(part * CHAN, (part + 1) * CHAN)
        w_copies.append(
            pltpu.make_async_copy(w_hbm.at[:, cols], w.at[:, cols], local_sem.at[1 + part])
        )
        w_copies[-1].start()

    barrier = pltpu.get_barrier_semaphore()
    for device in (up, down, left, right):
        pl.semaphore_signal(barrier, inc=1, device_id=device, device_id_type=MESH)
    own_copy.wait()
    for row in range(16):
        edge_l[8 * row : 8 * row + 8] = xm[4 + row, 0:8]
        edge_r[8 * row : 8 * row + 8] = xm[4 + row, 8:16]
    pl.semaphore_wait(barrier, 4)

    def send(index, src, dst, device):
        copy = pltpu.make_async_remote_copy(
            src_ref=src,
            dst_ref=dst,
            send_sem=send_sem.at[index],
            recv_sem=recv_sem.at[index],
            device_id=device,
            device_id_type=MESH,
        )
        copy.start()
        return copy

    to_left = send(0, edge_l, xr.at[32:160], left)
    to_right = send(1, edge_r, xl.at[32:160], right)
    to_up = send(2, xm.at[4:8], xm.at[20:24], up)
    to_down = send(3, xm.at[16:20], xm.at[0:4], down)

    dk[...] = jnp.zeros_like(dk)
    dv[...] = jnp.zeros_like(dv)

    first_row = lat * 16
    height = n_lat * 16
    lane = lax.broadcasted_iota(jnp.int32, (1, 128), 1)
    q_row, q_col = lane % 64 // 16, lane % 16
    cell = lax.broadcasted_iota(jnp.int32, (384, 1), 0)
    k_row, k_pos = cell // 32, cell % 32
    k_col = jnp.where(k_pos < 16, k_pos, jnp.where(k_pos < 24, k_pos - 24, k_pos - 8))
    row_gap = jnp.abs(k_row - RMAX - q_row)
    col_gap = jnp.abs(k_col - q_col)
    for b in range(4):
        reach_r = jnp.zeros((1, 128), jnp.int32)
        reach_c = jnp.zeros((1, 128), jnp.int32)
        for row in range(4):
            reach_r = jnp.where(q_row == row, rr_ref[first_row + 4 * b + row], reach_r)
            reach_c = jnp.where(q_row == row, cc_ref[first_row + 4 * b + row], reach_c)
        key_row = first_row + 4 * b - RMAX + k_row
        ok = (row_gap <= reach_r) & (col_gap <= reach_c) & ((key_row >= 0) & (key_row < height))
        bias[b] = jnp.where(ok, 0.0, -1e30)

    for copy in w_copies:
        copy.wait()

    def w_cols(part, i):
        return w[:, pl.ds(pl.multiple_of(part * CHAN + i * GROUP, GROUP), GROUP)]

    def project_own(i, _):
        own = xm[4:20].reshape(256, CHAN)
        q[i] = dot(own, w_cols(0, i), NN).astype(BF16) * BF16(0.125)
        k[i, 4:20, 0:16] = dot(own, w_cols(1, i), NN).astype(BF16).reshape(16, 16, GROUP)
        v[i, 4:20, 0:16] = dot(own, w_cols(2, i), NN).astype(BF16).reshape(16, 16, GROUP)
        return 0

    lax.fori_loop(0, NGROUP, project_own, 0)

    to_left.wait_recv()
    to_right.wait_recv()
    corners = [
        send(4, xl.at[32:64], xl.at[160:192], up),
        send(5, xr.at[32:64], xr.at[160:192], up),
        send(6, xl.at[128:160], xl.at[0:32], down),
        send(7, xr.at[128:160], xr.at[0:32], down),
    ]

    def project_sides(i, _):
        for part, out in ((1, k), (2, v)):
            wt = w_cols(part, i)
            sides = jnp.concatenate([xl[32:160], xr[32:160]], 0)
            r = dot(sides, wt, NN).reshape(32, 8, GROUP).astype(BF16)
            out[i, 4:20, 16:24] = r[:16]
            out[i, 4:20, 24:32] = r[16:]
        return 0

    lax.fori_loop(0, NGROUP, project_sides, 0)

    to_up.wait_recv()
    to_down.wait_recv()
    for copy in corners:
        copy.wait_recv()

    def project_caps(i, _):
        for part, out in ((1, k), (2, v)):
            wt = w_cols(part, i)
            cells = jnp.concatenate(
                [xm[0:4].reshape(64, CHAN), xm[20:24].reshape(64, CHAN), xl[0:32], xl[160:192], xr[0:32], xr[160:192]], 0
            )
            r = dot(cells, wt, NN)
            mid = r[:128].astype(BF16).reshape(8, 16, GROUP)
            rim = r[128:].reshape(16, 8, GROUP).astype(BF16)
            out[i, 0:4, 0:16] = mid[:4]
            out[i, 20:24, 0:16] = mid[4:]
            out[i, 0:4, 16:24] = rim[0:4]
            out[i, 20:24, 16:24] = rim[4:8]
            out[i, 0:4, 24:32] = rim[8:12]
            out[i, 20:24, 24:32] = rim[12:16]
        return 0

    lax.fori_loop(0, NGROUP, project_caps, 0)

    def attend(b, hg):
        lanes = pl.ds(pl.multiple_of(hg * GROUP, GROUP), GROUP)
        window = slice(4 * b, 4 * b + 12)
        keys = k[hg, window].reshape(384, GROUP)
        vals = v[hg, window].reshape(384, GROUP)
        qd = block_diagonal(q[hg, 64 * b : 64 * b + 64])
        gd = block_diagonal(g_ref[4 * b : 4 * b + 4, :, lanes].reshape(64, GROUP))
        masked = bias[b]
        s = dot(keys, qd, NT) + jnp.concatenate([masked, masked], 1)
        e = jnp.exp(s - jnp.max(s, 0, keepdims=True))
        p = e * (1.0 / jnp.sum(e, 0, keepdims=True))
        dp = dot(vals, gd, NT)
        delta = jnp.sum(p * dp, 0, keepdims=True)
        ds = (p * (dp - delta)).astype(BF16)
        pb = p.astype(BF16)
        dk[hg, window] += dot(ds, qd, NN).reshape(12, 32, GROUP)
        dv[hg, window] += dot(pb, gd, NN).reshape(12, 32, GROUP)
        att_ref[64 * b : 64 * b + 64, lanes] = take_diagonal(dot(pb, vals, TN)).astype(BF16)
        dq[64 * b : 64 * b + 64, lanes] = (take_diagonal(dot(ds, keys, TN)) * 0.125).astype(BF16)

    def attend_block(b):
        def body(i, _):
            attend(b, 2 * i)
            attend(b, 2 * i + 1)
            return 0

        lax.fori_loop(0, NGROUP // 2, body, 0)

    attend_block(0)
    attend_block(3)

    for hg in range(NGROUP):
        for offset, src in ((CHAN, dk), (2 * CHAN, dv)):
            cols = slice(offset + hg * GROUP, offset + (hg + 1) * GROUP)
            grads[0:128, cols] = src[hg, 0:4].reshape(128, GROUP).astype(BF16)
            grads[128:256, cols] = src[hg, 20:24].reshape(128, GROUP).astype(BF16)

    def back_caps(n, _):
        lanes = pl.ds(pl.multiple_of(n * GROUP, GROUP), GROUP)
        r = dot(grads[:, CHAN:], w[lanes, CHAN:], NT).astype(BF16)
        tb_send[:, :, lanes] = r.reshape(8, 32, GROUP)
        return 0

    lax.fori_loop(0, NGROUP, back_caps, 0)
    back_up = send(8, tb_send.at[0:4], tb_recv.at[4:8], up)
    back_down = send(9, tb_send.at[4:8], tb_recv.at[0:4], down)

    attend_block(1)
    attend_block(2)

    for hg in range(NGROUP):
        for offset, src in ((CHAN, dk), (2 * CHAN, dv)):
            cols = slice(offset + hg * GROUP, offset + (hg + 1) * GROUP)
            grads[0:128, cols] = src[hg, 4:20, 16:24].reshape(128, GROUP).astype(BF16)
            grads[128:256, cols] = src[hg, 4:20, 24:32].reshape(128, GROUP).astype(BF16)
    back_up.wait_recv()
    back_down.wait_recv()

    def back_sides(n, _):
        lanes = pl.ds(pl.multiple_of(n * GROUP, GROUP), GROUP)
        r = dot(grads[:, CHAN:], w[lanes, CHAN:], NT)
        rim = tb_recv[:, 16:32, lanes].astype(F32)
        for side in range(2):
            half = r[128 * side : 128 * side + 128]
            part = rim[:, 8 * side : 8 * side + 8].reshape(64, GROUP)
            whole = jnp.concatenate([half[:32] + part[:32], half[32:96], half[96:] + part[32:]], 0)
            side_send[side, :, lanes] = whole.astype(BF16)
        return 0

    lax.fori_loop(0, NGROUP, back_sides, 0)
    back_left = send(10, side_send.at[0], side_recv.at[1], left)
    back_right = send(11, side_send.at[1], side_recv.at[0], right)

    grads[:, :CHAN] = dq[...]
    for hg in range(NGROUP):
        for offset, src in ((CHAN, dk), (2 * CHAN, dv)):
            cols = slice(offset + hg * GROUP, offset + (hg + 1) * GROUP)
            grads[:, cols] = src[hg, 4:20, 0:16].reshape(256, GROUP).astype(BF16)

    own_out = dk

    def back_own(n, _):
        lanes = pl.ds(pl.multiple_of(n * GROUP, GROUP), GROUP)
        r = dot(grads[...], w[lanes, :], NT)
        cap = tb_recv[:, 0:16, lanes].astype(F32).reshape(128, GROUP)
        whole = jnp.concatenate([r[:64] + cap[:64], r[64:192], r[192:] + cap[64:]], 0)
        own_out[n, 0:16, 0:16] = whole.reshape(16, 16, GROUP)
        return 0

    lax.fori_loop(0, NGROUP, back_own, 0)
    back_left.wait_recv()
    back_right.wait_recv()
    for n in range(NGROUP):
        lanes = slice(n * GROUP, (n + 1) * GROUP)
        for side in range(2):
            part = side_recv[side, :, lanes].astype(F32).reshape(16, 8, GROUP)
            own_out[n, 0:16, 8 * side : 8 * side + 8] += part
        fg_ref[:, lanes] = own_out[n, 0:16, 0:16].reshape(256, GROUP).astype(BF16)

    for copy in (to_left, to_right, to_up, to_down, *corners, back_up, back_down, back_left, back_right):
        copy.wait_send()


def shards(features, w_qkv, cotangent, row_reach, col_reach):
    vmem = pl.BlockSpec(memory_space=pltpu.VMEM)
    smem = pl.BlockSpec(memory_space=pltpu.SMEM)
    any_space = pl.BlockSpec(memory_space=pl.ANY)
    att, grad = pl.pallas_call(
        kernel,
        out_shape=[jax.ShapeDtypeStruct((256, CHAN), BF16)] * 2,
        in_specs=[any_space, any_space, vmem, smem, smem],
        out_specs=[vmem, vmem],
        scratch_shapes=[
            pltpu.VMEM((24, 16, CHAN), BF16),
            pltpu.VMEM((192, CHAN), BF16),
            pltpu.VMEM((192, CHAN), BF16),
            pltpu.VMEM((128, CHAN), BF16),
            pltpu.VMEM((128, CHAN), BF16),
            pltpu.VMEM((CHAN, 3 * CHAN), BF16),
            pltpu.VMEM((NGROUP, 256, GROUP), BF16),
            pltpu.VMEM((NGROUP, 24, 32, GROUP), BF16),
            pltpu.VMEM((NGROUP, 24, 32, GROUP), BF16),
            pltpu.VMEM((NGROUP, 24, 32, GROUP), F32),
            pltpu.VMEM((NGROUP, 24, 32, GROUP), F32),
            pltpu.VMEM((256, CHAN), BF16),
            pltpu.VMEM((4, 384, 128), F32),
            pltpu.VMEM((256, 3 * CHAN), BF16),
            pltpu.VMEM((8, 32, CHAN), BF16),
            pltpu.VMEM((8, 32, CHAN), BF16),
            pltpu.VMEM((2, 128, CHAN), BF16),
            pltpu.VMEM((2, 128, CHAN), BF16),
            pltpu.SemaphoreType.DMA((4,)),
            pltpu.SemaphoreType.DMA((12,)),
            pltpu.SemaphoreType.DMA((12,)),
        ],
        compiler_params=pltpu.CompilerParams(
            collective_id=0, has_side_effects=True, vmem_limit_bytes=56 << 20
        ),
        name="sphere_attention",
    )(features, w_qkv, cotangent, row_reach, col_reach)
    return att.reshape(features.shape), grad.reshape(features.shape)


def solution(mesh):
    placed = (P("lat", "lon", None), P(), P("lat", "lon", None), P(), P())
    return jax.shard_map(
        shards,
        mesh=mesh,
        in_specs=placed,
        out_specs=(P("lat", "lon", None), P("lat", "lon", None)),
        check_vma=False,
    )
```

```python
import jax
import jax.numpy as jnp
from jax import lax
from jax.experimental import pallas as pl
from jax.experimental.pallas import tpu as pltpu
from jax.sharding import PartitionSpec as P

HEADS = 16
RMAX = 4
CMAX = 8
CHAN = 1024
GROUP = 256
NGROUP = CHAN // GROUP
BLOCKS = 4
F32 = jnp.float32
BF16 = jnp.bfloat16
MESH = pl.DeviceIdType.MESH
NN = (((1,), (0,)), ((), ()))
NT = (((1,), (1,)), ((), ()))
TN = (((0,), (0,)), ((), ()))


def dot(a, b, dims):
    return lax.dot_general(a, b, dims, preferred_element_type=F32)


def block_diagonal(x):
    rows = lax.broadcasted_iota(jnp.int32, (256, GROUP), 0) // 64
    cols = lax.broadcasted_iota(jnp.int32, (256, GROUP), 1) // 64
    return jnp.where(rows == cols, jnp.concatenate([x] * 4, 0), jnp.zeros((), x.dtype))


def take_diagonal(o):
    cols = lax.broadcasted_iota(jnp.int32, (64, GROUP), 1) // 64
    out = o[:64]
    for head in range(1, 4):
        out = jnp.where(cols == head, o[64 * head : 64 * head + 64], out)
    return out


def kernel(
    x_hbm, w_hbm, g_hbm, rr_ref, cc_ref, att_ref, fg_ref,
    xm, xs, xc, edges, w, g, q, k, v, bias, probs, dscores,
    grads_cap, grads_side, grads_own, side_edge, own_out,
    cap_send, cap_recv, side_send, side_recv,
    local_sem, send_sem, recv_sem,
):
    lat, lon = lax.axis_index("lat"), lax.axis_index("lon")
    n_lat, n_lon = lax.axis_size("lat"), lax.axis_size("lon")
    up = (lax.rem(lat + n_lat - 1, n_lat), lon)
    down = (lax.rem(lat + 1, n_lat), lon)
    left = (lat, lax.rem(lon + n_lon - 1, n_lon))
    right = (lat, lax.rem(lon + 1, n_lon))

    barrier = pltpu.get_barrier_semaphore()
    for device in (up, down, left, right):
        pl.semaphore_signal(barrier, inc=1, device_id=device, device_id_type=MESH)

    def fetch(index, src, dst):
        copy = pltpu.make_async_copy(src, dst, local_sem.at[index])
        copy.start()
        return copy

    own_copy = fetch(0, x_hbm, xm)
    w_copies = []
    for part in range(3):
        cols = slice(part * CHAN, (part + 1) * CHAN)
        w_copies.append(fetch(1 + part, w_hbm.at[:, cols], w.at[:, cols]))
    g_copy = fetch(4, g_hbm, g)

    own_copy.wait()
    for row in range(16):
        edges[0, 8 * row : 8 * row + 8] = xm[16 * row : 16 * row + 8]
        edges[1, 8 * row : 8 * row + 8] = xm[16 * row + 8 : 16 * row + 16]
    pl.semaphore_wait(barrier, 4)

    sent = []

    def send(src, dst, device):
        index = len(sent)
        copy = pltpu.make_async_remote_copy(
            src_ref=src,
            dst_ref=dst,
            send_sem=send_sem.at[index],
            recv_sem=recv_sem.at[index],
            device_id=device,
            device_id_type=MESH,
        )
        copy.start()
        sent.append(copy)
        return copy

    to_left = send(edges.at[0], xs.at[128:256], left)
    to_right = send(edges.at[1], xs.at[0:128], right)
    to_up = send(xm.at[0:64], xc.at[64:128], up)
    to_down = send(xm.at[192:256], xc.at[0:64], down)

    first_row = lat * 16
    height = n_lat * 16
    lane = lax.broadcasted_iota(jnp.int32, (1, 128), 1)
    q_row, q_col = lane % 64 // 16, lane % 16
    cell = lax.broadcasted_iota(jnp.int32, (384, 1), 0)
    pair, place = cell // 64, cell % 64
    own = place < 32
    k_row = 2 * pair + jnp.where(own, place // 16, place % 16 // 8)
    k_col = jnp.where(own, place % 16, place % 8 + jnp.where(place < 48, -8, 16))
    row_gap = jnp.abs(k_row - RMAX - q_row)
    col_gap = jnp.abs(k_col - q_col)
    for b in range(BLOCKS):
        reach_r = jnp.zeros((1, 128), jnp.int32)
        reach_c = jnp.zeros((1, 128), jnp.int32)
        for row in range(4):
            reach_r = jnp.where(q_row == row, rr_ref[first_row + 4 * b + row], reach_r)
            reach_c = jnp.where(q_row == row, cc_ref[first_row + 4 * b + row], reach_c)
        key_row = first_row + 4 * b - RMAX + k_row
        ok = (row_gap <= reach_r) & (col_gap <= reach_c) & ((key_row >= 0) & (key_row < height))
        bias[b] = jnp.where(ok, 0.0, -1e30)

    def w_cols(part, i):
        return w[:, pl.ds(pl.multiple_of(part * CHAN + i * GROUP, GROUP), GROUP)]

    def project_query(i, _):
        r = dot(xm[...], w_cols(0, i), NN)
        q[i] = r.astype(BF16) * BF16(0.125)
        return 0

    def project_own(i, _):
        cells = xm[...]
        k[i, 2:10, 0:32] = dot(cells, w_cols(1, i), NN).astype(BF16).reshape(8, 32, GROUP)
        v[i, 2:10, 0:32] = dot(cells, w_cols(2, i), NN).astype(BF16).reshape(8, 32, GROUP)
        return 0

    w_copies[0].wait()
    lax.fori_loop(0, NGROUP, project_query, 0)
    w_copies[1].wait()
    w_copies[2].wait()
    lax.fori_loop(0, NGROUP, project_own, 0)

    to_left.wait_recv()
    to_right.wait_recv()
    corners = []
    for side in range(2):
        base = 128 * side
        corners.append(send(xs.at[base : base + 32], xc.at[160 + 64 * side : 192 + 64 * side], up))
        corners.append(send(xs.at[base + 96 : base + 128], xc.at[128 + 64 * side : 160 + 64 * side], down))

    def project_sides(i, _):
        for part, out in ((1, k), (2, v)):
            r = dot(xs[...], w_cols(part, i), NN).astype(BF16).reshape(16, 16, GROUP)
            out[i, 2:10, 32:48] = r[:8]
            out[i, 2:10, 48:64] = r[8:]
        return 0

    lax.fori_loop(0, NGROUP, project_sides, 0)
    g_copy.wait()

    def query_block(b, hg):
        return block_diagonal(q[hg, pl.ds(64 * b, 64)])

    def grad_block(b, hg):
        lanes = slice(hg * GROUP, (hg + 1) * GROUP) if isinstance(hg, int) else pl.ds(pl.multiple_of(hg * GROUP, GROUP), GROUP)
        return block_diagonal(g[pl.ds(4 * b, 4), :, lanes].reshape(64, GROUP))

    def attend(b, hg):
        keys = k[hg, pl.ds(2 * b, 6)].reshape(384, GROUP)
        vals = v[hg, pl.ds(2 * b, 6)].reshape(384, GROUP)
        masked = bias[b]
        s = dot(keys, query_block(b, hg), NT) + jnp.concatenate([masked, masked], 1)
        e = jnp.exp(s - jnp.max(s, 0, keepdims=True))
        p = e * (1.0 / jnp.sum(e, 0, keepdims=True))
        dp = dot(vals, grad_block(b, hg), NT)
        delta = jnp.sum(p * dp, 0, keepdims=True)
        dscores[b, hg] = (p * (dp - delta)).astype(BF16)
        probs[b, hg] = p.astype(BF16)

    def attend_block(b):
        for hg in range(NGROUP):
            attend(b, hg)

    attend_block(1)

    to_up.wait_recv()
    to_down.wait_recv()
    for copy in corners:
        copy.wait_recv()

    def project_caps(i, _):
        for part, out in ((1, k), (2, v)):
            r = dot(xc[...], w_cols(part, i), NN).astype(BF16)
            own = r[:128].reshape(4, 32, GROUP)
            rim = r[128:].reshape(8, 16, GROUP)
            for end in range(2):
                rows = slice(10 * end, 10 * end + 2)
                out[i, rows, 0:32] = own[2 * end : 2 * end + 2]
                out[i, rows, 32:48] = rim[2 * end : 2 * end + 2]
                out[i, rows, 48:64] = rim[4 + 2 * end : 6 + 2 * end]
        return 0

    lax.fori_loop(0, NGROUP, project_caps, 0)
    attend_block(0)
    attend_block(3)

    tensors = ((dscores, query_block), (probs, grad_block))

    def grad_caps(hg, _):
        for index, (weights, block) in enumerate(tensors):
            lanes = pl.ds(pl.multiple_of(index * CHAN + hg * GROUP, GROUP), GROUP)
            for end, b in ((0, 0), (1, 3)):
                r = dot(weights[b, hg, 256 * end : 256 * end + 128], block(b, hg), NN).astype(BF16)
                for dst, src, size in ((0, 0, 32), (32, 64, 32), (64, 32, 16), (80, 96, 16), (96, 48, 16), (112, 112, 16)):
                    grads_cap[128 * end + dst : 128 * end + dst + size, lanes] = r[src : src + size]
        return 0

    lax.fori_loop(0, NGROUP, grad_caps, 0)

    def back_caps(n, _):
        lanes = pl.ds(pl.multiple_of(n * GROUP, GROUP), GROUP)
        cap_send[:, lanes] = dot(grads_cap[...], w[lanes, CHAN:], NT).astype(BF16)
        return 0

    lax.fori_loop(0, NGROUP, back_caps, 0)
    back_up = send(cap_send.at[0:128], cap_recv.at[128:256], up)
    back_down = send(cap_send.at[128:256], cap_recv.at[0:128], down)

    attend_block(2)

    def window_sums(weights, block, hg, start, size):
        parts = []
        for b in range(BLOCKS):
            rows = weights[b, hg].reshape(6, 64, GROUP)[:, start : start + size].reshape(6 * size, GROUP)
            parts.append(dot(rows, block(b, hg), NN))
        sums = []
        for p in range(2, 10):
            terms = [parts[b][(p - 2 * b) * size : (p - 2 * b + 1) * size] for b in range(BLOCKS) if 0 <= p - 2 * b < 6]
            sums.append(sum(terms[1:], terms[0]))
        return sums

    def grad_sides(hg, _):
        for index, (weights, block) in enumerate(tensors):
            lanes = pl.ds(pl.multiple_of(index * CHAN + hg * GROUP, GROUP), GROUP)
            sums = window_sums(weights, block, hg, 32, 32)
            for slot, p in enumerate((0, 1, 6, 7, 2, 3, 4, 5)):
                r = sums[p].astype(BF16)
                grads_side[16 * slot : 16 * slot + 16, lanes] = r[:16]
                grads_side[128 + 16 * slot : 144 + 16 * slot, lanes] = r[16:]
        return 0

    lax.fori_loop(0, NGROUP, grad_sides, 0)

    def back_sides(n, _):
        lanes = pl.ds(pl.multiple_of(n * GROUP, GROUP), GROUP)
        r = dot(grads_side[...], w[lanes, CHAN:], NT)
        for side in range(2):
            side_edge[side, :, lanes] = r[128 * side : 128 * side + 64]
            side_send[side, 64:128, lanes] = r[128 * side + 64 : 128 * side + 128].astype(BF16)
        return 0

    lax.fori_loop(0, NGROUP, back_sides, 0)
    returns = [
        send(side_send.at[0, 64:128], side_recv.at[1, 64:128], left),
        send(side_send.at[1, 64:128], side_recv.at[0, 64:128], right),
    ]

    def grad_own(hg, _):
        for index, (weights, block) in enumerate(tensors):
            lanes = pl.ds(pl.multiple_of((1 + index) * CHAN + hg * GROUP, GROUP), GROUP)
            for p, r in enumerate(window_sums(weights, block, hg, 0, 32)):
                grads_own[32 * p : 32 * p + 32, lanes] = r.astype(BF16)
        return 0

    lax.fori_loop(0, NGROUP, grad_own, 0)

    def outputs(b, _):
        rows = pl.ds(64 * b, 64)
        for hg in range(NGROUP):
            lanes = slice(hg * GROUP, (hg + 1) * GROUP)
            keys = k[hg, pl.ds(2 * b, 6)].reshape(384, GROUP)
            vals = v[hg, pl.ds(2 * b, 6)].reshape(384, GROUP)
            att_ref[rows, lanes] = take_diagonal(dot(probs[b, hg], vals, TN)).astype(BF16)
            grads_own[rows, lanes] = (take_diagonal(dot(dscores[b, hg], keys, TN)) * 0.125).astype(BF16)
        return 0

    lax.fori_loop(0, 2, outputs, 0)

    back_up.wait_recv()
    back_down.wait_recv()
    for side in range(2):
        for end in range(2):
            rows = slice(32 * end, 32 * end + 32)
            rim = slice(128 * end + 64 + 32 * side, 128 * end + 96 + 32 * side)
            side_send[side, rows] = (side_edge[side, rows] + cap_recv[rim].astype(F32)).astype(BF16)
    returns.append(send(side_send.at[0, 0:64], side_recv.at[1, 0:64], left))
    returns.append(send(side_send.at[1, 0:64], side_recv.at[0, 0:64], right))

    lax.fori_loop(2, BLOCKS, outputs, 0)

    def back_own(n, _):
        lanes = pl.ds(pl.multiple_of(n * GROUP, GROUP), GROUP)
        r = dot(grads_own[...], w[lanes, :], NT)
        own_out[0:64, lanes] = r[:64] + cap_recv[0:64, lanes].astype(F32)
        own_out[64:192, lanes] = r[64:192]
        own_out[192:256, lanes] = r[192:] + cap_recv[128:192, lanes].astype(F32)
        return 0

    lax.fori_loop(0, NGROUP, back_own, 0)
    for copy in returns:
        copy.wait_recv()
    for slot, row in enumerate((0, 1, 2, 3, 12, 13, 14, 15, 4, 5, 6, 7, 8, 9, 10, 11)):
        both = jnp.concatenate([side_recv[side, 8 * slot : 8 * slot + 8].astype(F32) for side in range(2)], 0)
        rows = slice(16 * row, 16 * row + 16)
        fg_ref[rows] = (own_out[rows] + both).astype(BF16)

    for copy in sent:
        copy.wait_send()


def hand_over(att_ref, grad_ref, att_out, grad_out, held, in_sem, out_sem):
    parts = []
    for index, (src, dst) in enumerate(((att_ref, att_out), (grad_ref, grad_out))):
        for part in range(4):
            rows, slot = slice(64 * part, 64 * part + 64), 4 * index + part
            fetch = pltpu.make_async_copy(src.at[rows], held.at[slot], in_sem.at[slot])
            store = pltpu.make_async_copy(held.at[slot], dst.at[rows], out_sem.at[slot])
            fetch.start()
            parts.append((fetch, store))
    for fetch, store in parts:
        fetch.wait()
        store.start()
    for _, store in parts:
        store.wait()


def shards(features, w_qkv, cotangent, row_reach, col_reach):
    vmem = pl.BlockSpec(memory_space=pltpu.VMEM)
    smem = pl.BlockSpec(memory_space=pltpu.SMEM)
    any_space = pl.BlockSpec(memory_space=pl.ANY)
    flat = [jax.ShapeDtypeStruct((256, CHAN), BF16)] * 2
    att, grad = pl.pallas_call(
        kernel,
        out_shape=flat,
        in_specs=[any_space, any_space, any_space, smem, smem],
        out_specs=[vmem, vmem],
        scratch_shapes=[
            pltpu.VMEM((256, CHAN), BF16),
            pltpu.VMEM((256, CHAN), BF16),
            pltpu.VMEM((256, CHAN), BF16),
            pltpu.VMEM((2, 128, CHAN), BF16),
            pltpu.VMEM((CHAN, 3 * CHAN), BF16),
            pltpu.VMEM((16, 16, CHAN), BF16),
            pltpu.VMEM((NGROUP, 256, GROUP), BF16),
            pltpu.VMEM((NGROUP, 12, 64, GROUP), BF16),
            pltpu.VMEM((NGROUP, 12, 64, GROUP), BF16),
            pltpu.VMEM((BLOCKS, 384, 128), F32),
            pltpu.VMEM((BLOCKS, NGROUP, 384, GROUP), BF16),
            pltpu.VMEM((BLOCKS, NGROUP, 384, GROUP), BF16),
            pltpu.VMEM((256, 2 * CHAN), BF16),
            pltpu.VMEM((256, 2 * CHAN), BF16),
            pltpu.VMEM((256, 3 * CHAN), BF16),
            pltpu.VMEM((2, 64, CHAN), F32),
            pltpu.VMEM((256, CHAN), F32),
            pltpu.VMEM((256, CHAN), BF16),
            pltpu.VMEM((256, CHAN), BF16),
            pltpu.VMEM((2, 128, CHAN), BF16),
            pltpu.VMEM((2, 128, CHAN), BF16),
            pltpu.SemaphoreType.DMA((5,)),
            pltpu.SemaphoreType.DMA((14,)),
            pltpu.SemaphoreType.DMA((14,)),
        ],
        compiler_params=pltpu.CompilerParams(
            collective_id=0, has_side_effects=True, vmem_limit_bytes=56 << 20
        ),
        name="sphere_attention",
    )(features.reshape(256, CHAN), w_qkv, cotangent, row_reach, col_reach)
    att, grad = pl.pallas_call(
        hand_over,
        out_shape=flat,
        in_specs=[any_space, any_space],
        out_specs=[any_space, any_space],
        scratch_shapes=[
            pltpu.VMEM((8, 64, CHAN), BF16),
            pltpu.SemaphoreType.DMA((8,)),
            pltpu.SemaphoreType.DMA((8,)),
        ],
        name="hand_over",
    )(att, grad)
    return att.reshape(features.shape), grad.reshape(features.shape)


def solution(mesh):
    placed = (P("lat", "lon", None), P(), P("lat", "lon", None), P(), P())
    return jax.shard_map(
        shards,
        mesh=mesh,
        in_specs=placed,
        out_specs=(P("lat", "lon", None), P("lat", "lon", None)),
        check_vma=False,
    )
```

```python
import jax
import jax.numpy as jnp
from jax import lax
from jax.experimental import pallas as pl
from jax.experimental.pallas import tpu as pltpu
from jax.sharding import PartitionSpec as P

HEADS = 16
RMAX = 4
CMAX = 8
CHAN = 1024
GROUP = 256
NGROUP = CHAN // GROUP
BLOCKS = 4
F32 = jnp.float32
BF16 = jnp.bfloat16
MESH = pl.DeviceIdType.MESH
NN = (((1,), (0,)), ((), ()))
NT = (((1,), (1,)), ((), ()))
TN = (((0,), (0,)), ((), ()))


def dot(a, b, dims):
    return lax.dot_general(a, b, dims, preferred_element_type=F32)


def block_diagonal(x):
    rows = lax.broadcasted_iota(jnp.int32, (256, GROUP), 0) // 64
    cols = lax.broadcasted_iota(jnp.int32, (256, GROUP), 1) // 64
    return jnp.where(rows == cols, jnp.concatenate([x] * 4, 0), jnp.zeros((), x.dtype))


def take_diagonal(o):
    cols = lax.broadcasted_iota(jnp.int32, (64, GROUP), 1) // 64
    out = o[:64]
    for head in range(1, 4):
        out = jnp.where(cols == head, o[64 * head : 64 * head + 64], out)
    return out


def looped(body, count, unroll):
    def step(i, carry):
        for j in range(unroll):
            body(i * unroll + j, carry)
        return carry

    if unroll == count:
        step(0, 0)
    else:
        lax.fori_loop(0, count // unroll, step, 0)


def kernel(
    x_hbm, w_hbm, g_hbm, rr_ref, cc_ref, att_ref, fg_ref,
    xm, xs, xc, edges, w, g, q, k, v, bias, probs, dscores,
    grads_cap, grads_side, grads_own, side_edge, own_out,
    cap_send, cap_recv, side_send, side_recv,
    local_sem, send_sem, recv_sem,
):
    lat, lon = lax.axis_index("lat"), lax.axis_index("lon")
    n_lat, n_lon = lax.axis_size("lat"), lax.axis_size("lon")
    up = (lax.rem(lat + n_lat - 1, n_lat), lon)
    down = (lax.rem(lat + 1, n_lat), lon)
    left = (lat, lax.rem(lon + n_lon - 1, n_lon))
    right = (lat, lax.rem(lon + 1, n_lon))

    barrier = pltpu.get_barrier_semaphore()
    for device in (up, down, left, right):
        pl.semaphore_signal(barrier, inc=1, device_id=device, device_id_type=MESH)

    def fetch(index, src, dst):
        copy = pltpu.make_async_copy(src, dst, local_sem.at[index])
        copy.start()
        return copy

    own_copy = fetch(0, x_hbm, xm)
    w_copies = []
    for part in range(3):
        cols = slice(part * CHAN, (part + 1) * CHAN)
        w_copies.append(fetch(1 + part, w_hbm.at[:, cols], w.at[:, cols]))
    g_copy = fetch(4, g_hbm, g)

    own_copy.wait()
    for row in range(16):
        edges[0, 8 * row : 8 * row + 8] = xm[16 * row : 16 * row + 8]
        edges[1, 8 * row : 8 * row + 8] = xm[16 * row + 8 : 16 * row + 16]
    pl.semaphore_wait(barrier, 4)

    sent = []

    def send(src, dst, device):
        index = len(sent)
        copy = pltpu.make_async_remote_copy(
            src_ref=src,
            dst_ref=dst,
            send_sem=send_sem.at[index],
            recv_sem=recv_sem.at[index],
            device_id=device,
            device_id_type=MESH,
        )
        copy.start()
        sent.append(copy)
        return copy

    to_left = send(edges.at[0], xs.at[128:256], left)
    to_right = send(edges.at[1], xs.at[0:128], right)
    to_up = send(xm.at[0:64], xc.at[64:128], up)
    to_down = send(xm.at[192:256], xc.at[0:64], down)

    first_row = lat * 16
    height = n_lat * 16
    lane = lax.broadcasted_iota(jnp.int32, (1, 128), 1)
    q_row, q_col = lane % 64 // 16, lane % 16
    cell = lax.broadcasted_iota(jnp.int32, (384, 1), 0)
    pair, place = cell // 64, cell % 64
    own = place < 32
    k_row = 2 * pair + jnp.where(own, place // 16, place % 16 // 8)
    k_col = jnp.where(own, place % 16, place % 8 + jnp.where(place < 48, -8, 16))
    row_gap = jnp.abs(k_row - RMAX - q_row)
    col_gap = jnp.abs(k_col - q_col)
    for b in range(BLOCKS):
        reach_r = jnp.zeros((1, 128), jnp.int32)
        reach_c = jnp.zeros((1, 128), jnp.int32)
        for row in range(4):
            reach_r = jnp.where(q_row == row, rr_ref[first_row + 4 * b + row], reach_r)
            reach_c = jnp.where(q_row == row, cc_ref[first_row + 4 * b + row], reach_c)
        key_row = first_row + 4 * b - RMAX + k_row
        ok = (row_gap <= reach_r) & (col_gap <= reach_c) & ((key_row >= 0) & (key_row < height))
        bias[b] = jnp.where(ok, 0.0, -1e30)

    def w_cols(part, i):
        return w[:, pl.ds(pl.multiple_of(part * CHAN + i * GROUP, GROUP), GROUP)]

    def project_query(i, _):
        r = dot(xm[...], w_cols(0, i), NN)
        q[i] = r.astype(BF16) * BF16(0.125)
        return 0

    def project_own(i, _):
        cells = xm[...]
        k[i, 2:10, 0:32] = dot(cells, w_cols(1, i), NN).astype(BF16).reshape(8, 32, GROUP)
        v[i, 2:10, 0:32] = dot(cells, w_cols(2, i), NN).astype(BF16).reshape(8, 32, GROUP)
        return 0

    w_copies[0].wait()
    looped(project_query, NGROUP, 4)
    w_copies[1].wait()
    w_copies[2].wait()
    looped(project_own, NGROUP, 4)

    to_left.wait_recv()
    to_right.wait_recv()
    corners = []
    for side in range(2):
        base = 128 * side
        corners.append(send(xs.at[base : base + 32], xc.at[160 + 64 * side : 192 + 64 * side], up))
        corners.append(send(xs.at[base + 96 : base + 128], xc.at[128 + 64 * side : 160 + 64 * side], down))

    def project_sides(i, _):
        for part, out in ((1, k), (2, v)):
            r = dot(xs[...], w_cols(part, i), NN).astype(BF16).reshape(16, 16, GROUP)
            out[i, 2:10, 32:48] = r[:8]
            out[i, 2:10, 48:64] = r[8:]
        return 0

    looped(project_sides, NGROUP, 4)
    g_copy.wait()

    def query_block(b, hg):
        return block_diagonal(q[hg, pl.ds(64 * b, 64)])

    def grad_block(b, hg):
        lanes = slice(hg * GROUP, (hg + 1) * GROUP) if isinstance(hg, int) else pl.ds(pl.multiple_of(hg * GROUP, GROUP), GROUP)
        return block_diagonal(g[pl.ds(4 * b, 4), :, lanes].reshape(64, GROUP))

    def attend(b, hg):
        keys = k[hg, pl.ds(2 * b, 6)].reshape(384, GROUP)
        vals = v[hg, pl.ds(2 * b, 6)].reshape(384, GROUP)
        masked = bias[b]
        s = dot(keys, query_block(b, hg), NT) + jnp.concatenate([masked, masked], 1)
        e = jnp.exp(s - jnp.max(s, 0, keepdims=True))
        p = e * (1.0 / jnp.sum(e, 0, keepdims=True))
        dp = dot(vals, grad_block(b, hg), NT)
        delta = jnp.sum(p * dp, 0, keepdims=True)
        dscores[b, hg] = (p * (dp - delta)).astype(BF16)
        probs[b, hg] = p.astype(BF16)

    def attend_block(b):
        for hg in range(NGROUP):
            attend(b, hg)

    attend_block(1)

    to_up.wait_recv()
    to_down.wait_recv()
    for copy in corners:
        copy.wait_recv()

    def project_caps(i, _):
        for part, out in ((1, k), (2, v)):
            r = dot(xc[...], w_cols(part, i), NN).astype(BF16)
            own = r[:128].reshape(4, 32, GROUP)
            rim = r[128:].reshape(8, 16, GROUP)
            for end in range(2):
                rows = slice(10 * end, 10 * end + 2)
                out[i, rows, 0:32] = own[2 * end : 2 * end + 2]
                out[i, rows, 32:48] = rim[2 * end : 2 * end + 2]
                out[i, rows, 48:64] = rim[4 + 2 * end : 6 + 2 * end]
        return 0

    looped(project_caps, NGROUP, 4)
    attend_block(0)
    attend_block(3)

    tensors = ((dscores, query_block), (probs, grad_block))

    def grad_caps(hg, _):
        for index, (weights, block) in enumerate(tensors):
            lanes = pl.ds(pl.multiple_of(index * CHAN + hg * GROUP, GROUP), GROUP)
            for end, b in ((0, 0), (1, 3)):
                r = dot(weights[b, hg, 256 * end : 256 * end + 128], block(b, hg), NN).astype(BF16)
                for dst, src, size in ((0, 0, 32), (32, 64, 32), (64, 32, 16), (80, 96, 16), (96, 48, 16), (112, 112, 16)):
                    grads_cap[128 * end + dst : 128 * end + dst + size, lanes] = r[src : src + size]
        return 0

    looped(grad_caps, NGROUP, 4)

    def back_caps(n, _):
        lanes = pl.ds(pl.multiple_of(n * GROUP, GROUP), GROUP)
        cap_send[:, lanes] = dot(grads_cap[...], w[lanes, CHAN:], NT).astype(BF16)
        return 0

    looped(back_caps, NGROUP, 4)
    back_up = send(cap_send.at[0:128], cap_recv.at[128:256], up)
    back_down = send(cap_send.at[128:256], cap_recv.at[0:128], down)

    attend_block(2)

    def window_sums(weights, block, hg, start, size):
        parts = []
        for b in range(BLOCKS):
            rows = weights[b, hg].reshape(6, 64, GROUP)[:, start : start + size].reshape(6 * size, GROUP)
            parts.append(dot(rows, block(b, hg), NN))
        sums = []
        for p in range(2, 10):
            terms = [parts[b][(p - 2 * b) * size : (p - 2 * b + 1) * size] for b in range(BLOCKS) if 0 <= p - 2 * b < 6]
            sums.append(sum(terms[1:], terms[0]))
        return sums

    def grad_sides(hg, _):
        for index, (weights, block) in enumerate(tensors):
            lanes = pl.ds(pl.multiple_of(index * CHAN + hg * GROUP, GROUP), GROUP)
            sums = window_sums(weights, block, hg, 32, 32)
            for slot, p in enumerate((0, 1, 6, 7, 2, 3, 4, 5)):
                r = sums[p].astype(BF16)
                grads_side[16 * slot : 16 * slot + 16, lanes] = r[:16]
                grads_side[128 + 16 * slot : 144 + 16 * slot, lanes] = r[16:]
        return 0

    looped(grad_sides, NGROUP, 4)

    def back_sides(n, _):
        lanes = pl.ds(pl.multiple_of(n * GROUP, GROUP), GROUP)
        r = dot(grads_side[...], w[lanes, CHAN:], NT)
        for side in range(2):
            side_edge[side, :, lanes] = r[128 * side : 128 * side + 64]
            side_send[side, 64:128, lanes] = r[128 * side + 64 : 128 * side + 128].astype(BF16)
        return 0

    looped(back_sides, NGROUP, 4)
    returns = [
        send(side_send.at[0, 64:128], side_recv.at[1, 64:128], left),
        send(side_send.at[1, 64:128], side_recv.at[0, 64:128], right),
    ]

    def grad_own(hg, _):
        for index, (weights, block) in enumerate(tensors):
            lanes = pl.ds(pl.multiple_of((1 + index) * CHAN + hg * GROUP, GROUP), GROUP)
            for p, r in enumerate(window_sums(weights, block, hg, 0, 32)):
                grads_own[32 * p : 32 * p + 32, lanes] = r.astype(BF16)
        return 0

    looped(grad_own, NGROUP, 4)

    def outputs(b, _):
        rows = pl.ds(64 * b, 64)
        for hg in range(NGROUP):
            lanes = slice(hg * GROUP, (hg + 1) * GROUP)
            keys = k[hg, pl.ds(2 * b, 6)].reshape(384, GROUP)
            vals = v[hg, pl.ds(2 * b, 6)].reshape(384, GROUP)
            att_ref[rows, lanes] = take_diagonal(dot(probs[b, hg], vals, TN)).astype(BF16)
            grads_own[rows, lanes] = (take_diagonal(dot(dscores[b, hg], keys, TN)) * 0.125).astype(BF16)
        return 0

    lax.fori_loop(0, 2, outputs, 0)

    back_up.wait_recv()
    back_down.wait_recv()
    for side in range(2):
        for end in range(2):
            rows = slice(32 * end, 32 * end + 32)
            rim = slice(128 * end + 64 + 32 * side, 128 * end + 96 + 32 * side)
            side_send[side, rows] = (side_edge[side, rows] + cap_recv[rim].astype(F32)).astype(BF16)
    returns.append(send(side_send.at[0, 0:64], side_recv.at[1, 0:64], left))
    returns.append(send(side_send.at[1, 0:64], side_recv.at[0, 0:64], right))

    lax.fori_loop(2, BLOCKS, outputs, 0)

    def back_own(n, _):
        lanes = pl.ds(pl.multiple_of(n * GROUP, GROUP), GROUP)
        r = dot(grads_own[...], w[lanes, :], NT)
        own_out[0:64, lanes] = r[:64] + cap_recv[0:64, lanes].astype(F32)
        own_out[64:192, lanes] = r[64:192]
        own_out[192:256, lanes] = r[192:] + cap_recv[128:192, lanes].astype(F32)
        return 0

    looped(back_own, NGROUP, 4)
    for copy in returns:
        copy.wait_recv()
    for slot, row in enumerate((0, 1, 2, 3, 12, 13, 14, 15, 4, 5, 6, 7, 8, 9, 10, 11)):
        both = jnp.concatenate([side_recv[side, 8 * slot : 8 * slot + 8].astype(F32) for side in range(2)], 0)
        rows = slice(16 * row, 16 * row + 16)
        fg_ref[rows] = (own_out[rows] + both).astype(BF16)

    for copy in sent:
        copy.wait_send()


def hand_over(att_ref, grad_ref, att_out, grad_out, held, in_sem, out_sem):
    parts = []
    for index, (src, dst) in enumerate(((att_ref, att_out), (grad_ref, grad_out))):
        for part in range(4):
            rows, slot = slice(64 * part, 64 * part + 64), 4 * index + part
            fetch = pltpu.make_async_copy(src.at[rows], held.at[slot], in_sem.at[slot])
            store = pltpu.make_async_copy(held.at[slot], dst.at[rows], out_sem.at[slot])
            fetch.start()
            parts.append((fetch, store))
    for fetch, store in parts:
        fetch.wait()
        store.start()
    for _, store in parts:
        store.wait()


def shards(features, w_qkv, cotangent, row_reach, col_reach):
    vmem = pl.BlockSpec(memory_space=pltpu.VMEM)
    smem = pl.BlockSpec(memory_space=pltpu.SMEM)
    any_space = pl.BlockSpec(memory_space=pl.ANY)
    flat = [jax.ShapeDtypeStruct((256, CHAN), BF16)] * 2
    att, grad = pl.pallas_call(
        kernel,
        out_shape=flat,
        in_specs=[any_space, any_space, any_space, smem, smem],
        out_specs=[vmem, vmem],
        scratch_shapes=[
            pltpu.VMEM((256, CHAN), BF16),
            pltpu.VMEM((256, CHAN), BF16),
            pltpu.VMEM((256, CHAN), BF16),
            pltpu.VMEM((2, 128, CHAN), BF16),
            pltpu.VMEM((CHAN, 3 * CHAN), BF16),
            pltpu.VMEM((16, 16, CHAN), BF16),
            pltpu.VMEM((NGROUP, 256, GROUP), BF16),
            pltpu.VMEM((NGROUP, 12, 64, GROUP), BF16),
            pltpu.VMEM((NGROUP, 12, 64, GROUP), BF16),
            pltpu.VMEM((BLOCKS, 384, 128), F32),
            pltpu.VMEM((BLOCKS, NGROUP, 384, GROUP), BF16),
            pltpu.VMEM((BLOCKS, NGROUP, 384, GROUP), BF16),
            pltpu.VMEM((256, 2 * CHAN), BF16),
            pltpu.VMEM((256, 2 * CHAN), BF16),
            pltpu.VMEM((256, 3 * CHAN), BF16),
            pltpu.VMEM((2, 64, CHAN), F32),
            pltpu.VMEM((256, CHAN), F32),
            pltpu.VMEM((256, CHAN), BF16),
            pltpu.VMEM((256, CHAN), BF16),
            pltpu.VMEM((2, 128, CHAN), BF16),
            pltpu.VMEM((2, 128, CHAN), BF16),
            pltpu.SemaphoreType.DMA((5,)),
            pltpu.SemaphoreType.DMA((14,)),
            pltpu.SemaphoreType.DMA((14,)),
        ],
        compiler_params=pltpu.CompilerParams(
            collective_id=0, has_side_effects=True, vmem_limit_bytes=56 << 20
        ),
        name="sphere_attention",
    )(features.reshape(256, CHAN), w_qkv, cotangent, row_reach, col_reach)
    att, grad = pl.pallas_call(
        hand_over,
        out_shape=flat,
        in_specs=[any_space, any_space],
        out_specs=[any_space, any_space],
        scratch_shapes=[
            pltpu.VMEM((8, 64, CHAN), BF16),
            pltpu.SemaphoreType.DMA((8,)),
            pltpu.SemaphoreType.DMA((8,)),
        ],
        name="hand_over",
    )(att, grad)
    return att.reshape(features.shape), grad.reshape(features.shape)


def solution(mesh):
    placed = (P("lat", "lon", None), P(), P("lat", "lon", None), P(), P())
    return jax.shard_map(
        shards,
        mesh=mesh,
        in_specs=placed,
        out_specs=(P("lat", "lon", None), P("lat", "lon", None)),
        check_vma=False,
    )
```

```python
import jax
import jax.numpy as jnp
from jax import lax
from jax.experimental import pallas as pl
from jax.experimental.pallas import tpu as pltpu
from jax.sharding import PartitionSpec as P

HEADS = 16
RMAX = 4
CMAX = 8
CHAN = 1024
GROUP = 256
NGROUP = CHAN // GROUP
BLOCKS = 4
OUTER_FIRST = (0, 1, 2, 3, 12, 13, 14, 15, 4, 5, 6, 7, 8, 9, 10, 11)
F32 = jnp.float32
BF16 = jnp.bfloat16
MESH = pl.DeviceIdType.MESH
NN = (((1,), (0,)), ((), ()))
NT = (((1,), (1,)), ((), ()))
TN = (((0,), (0,)), ((), ()))


def dot(a, b, dims):
    return lax.dot_general(a, b, dims, preferred_element_type=F32)


def block_diagonal(x):
    rows = lax.broadcasted_iota(jnp.int32, (256, GROUP), 0) // 64
    cols = lax.broadcasted_iota(jnp.int32, (256, GROUP), 1) // 64
    return jnp.where(rows == cols, jnp.concatenate([x] * 4, 0), jnp.zeros((), x.dtype))


def take_diagonal(o):
    cols = lax.broadcasted_iota(jnp.int32, (64, GROUP), 1) // 64
    out = o[:64]
    for head in range(1, 4):
        out = jnp.where(cols == head, o[64 * head : 64 * head + 64], out)
    return out


def looped(body, count, unroll):
    def step(i, carry):
        for j in range(unroll):
            body(i * unroll + j, carry)
        return carry

    if unroll == count:
        step(0, 0)
    else:
        lax.fori_loop(0, count // unroll, step, 0)


def kernel(
    x_hbm, w_hbm, g_hbm, rr_ref, cc_ref, att_out, grad_out,
    xm, xh, edges, w, g, q, k, v, bias, probs, dscores,
    grads_cap, grads_side, grads_own, side_edge, own_out,
    cap_send, cap_recv, side_send, side_recv, att_ref, fg_ref,
    local_sem, send_sem, recv_sem,
):
    lat, lon = lax.axis_index("lat"), lax.axis_index("lon")
    n_lat, n_lon = lax.axis_size("lat"), lax.axis_size("lon")
    up = (lax.rem(lat + n_lat - 1, n_lat), lon)
    down = (lax.rem(lat + 1, n_lat), lon)
    left = (lat, lax.rem(lon + n_lon - 1, n_lon))
    right = (lat, lax.rem(lon + 1, n_lon))

    barrier = pltpu.get_barrier_semaphore()
    for device in (up, down, left, right):
        pl.semaphore_signal(barrier, inc=1, device_id=device, device_id_type=MESH)

    def fetch(index, src, dst):
        copy = pltpu.make_async_copy(src, dst, local_sem.at[index])
        copy.start()
        return copy

    own_copy = fetch(0, x_hbm, xm)
    w_copies = []
    for part in range(3):
        cols = slice(part * CHAN, (part + 1) * CHAN)
        w_copies.append(fetch(1 + part, w_hbm.at[:, cols], w.at[:, cols]))
    g_copy = fetch(4, g_hbm, g)

    own_copy.wait()
    for slot, row in enumerate(OUTER_FIRST):
        edges[0, 8 * slot : 8 * slot + 8] = xm[16 * row : 16 * row + 8]
        edges[1, 8 * slot : 8 * slot + 8] = xm[16 * row + 8 : 16 * row + 16]
    pl.semaphore_wait(barrier, 4)

    sent = []

    def send(src, dst, device):
        index = len(sent)
        copy = pltpu.make_async_remote_copy(
            src_ref=src,
            dst_ref=dst,
            send_sem=send_sem.at[index],
            recv_sem=recv_sem.at[index],
            device_id=device,
            device_id_type=MESH,
        )
        copy.start()
        sent.append(copy)
        return copy

    near = [
        send(edges.at[0, 0:64], xh.at[64:128], left),
        send(edges.at[1, 0:64], xh.at[0:64], right),
        send(xm.at[0:64], xh.at[192:256], up),
        send(xm.at[192:256], xh.at[128:192], down),
    ]
    far = [
        send(edges.at[0, 64:128], xh.at[320:384], left),
        send(edges.at[1, 64:128], xh.at[256:320], right),
    ]

    first_row = lat * 16
    height = n_lat * 16
    lane = lax.broadcasted_iota(jnp.int32, (1, 128), 1)
    q_row, q_col = lane % 64 // 16, lane % 16
    cell = lax.broadcasted_iota(jnp.int32, (384, 1), 0)
    pair, place = cell // 64, cell % 64
    own = place < 32
    k_row = 2 * pair + jnp.where(own, place // 16, place % 16 // 8)
    k_col = jnp.where(own, place % 16, place % 8 + jnp.where(place < 48, -8, 16))
    row_gap = jnp.abs(k_row - RMAX - q_row)
    col_gap = jnp.abs(k_col - q_col)
    for b in range(BLOCKS):
        reach_r = jnp.zeros((1, 128), jnp.int32)
        reach_c = jnp.zeros((1, 128), jnp.int32)
        for row in range(4):
            reach_r = jnp.where(q_row == row, rr_ref[first_row + 4 * b + row], reach_r)
            reach_c = jnp.where(q_row == row, cc_ref[first_row + 4 * b + row], reach_c)
        key_row = first_row + 4 * b - RMAX + k_row
        ok = (row_gap <= reach_r) & (col_gap <= reach_c) & ((key_row >= 0) & (key_row < height))
        bias[b] = jnp.where(ok, 0.0, -1e30)

    def w_cols(part, i):
        return w[:, pl.ds(pl.multiple_of(part * CHAN + i * GROUP, GROUP), GROUP)]

    def project_query(i, _):
        r = dot(xm[...], w_cols(0, i), NN)
        q[i] = r.astype(BF16) * BF16(0.125)
        return 0

    def project_own(part, out):
        def project(i, _):
            r = dot(xm[...], w_cols(part, i), NN).astype(BF16)
            out[i, 2:10, 0:32] = r.reshape(8, 32, GROUP)
            return 0

        looped(project, NGROUP, 4)

    w_copies[0].wait()
    looped(project_query, NGROUP, 4)
    w_copies[1].wait()
    project_own(1, k)
    for copy in near:
        copy.wait_recv()
    for side in range(2):
        rows = 64 * side
        far.append(send(xh.at[rows : rows + 32], xh.at[416 + rows : 448 + rows], up))
        far.append(send(xh.at[rows + 32 : rows + 64], xh.at[384 + rows : 416 + rows], down))
    w_copies[2].wait()
    project_own(2, v)

    def project_near(i, _):
        for part, out in ((1, k), (2, v)):
            r = dot(xh[0:256], w_cols(part, i), NN).astype(BF16)
            for end, rows in ((0, slice(2, 4)), (1, slice(8, 10))):
                out[i, rows, 32:48] = r[32 * end : 32 * end + 32].reshape(2, 16, GROUP)
                out[i, rows, 48:64] = r[64 + 32 * end : 96 + 32 * end].reshape(2, 16, GROUP)
            out[i, 0:2, 0:32] = r[128:192].reshape(2, 32, GROUP)
            out[i, 10:12, 0:32] = r[192:256].reshape(2, 32, GROUP)
        return 0

    def project_far(i, _):
        for part, out in ((1, k), (2, v)):
            r = dot(xh[256:512], w_cols(part, i), NN).astype(BF16)
            out[i, 4:8, 32:48] = r[0:64].reshape(4, 16, GROUP)
            out[i, 4:8, 48:64] = r[64:128].reshape(4, 16, GROUP)
            for end, rows in ((0, slice(0, 2)), (1, slice(10, 12))):
                out[i, rows, 32:48] = r[128 + 32 * end : 160 + 32 * end].reshape(2, 16, GROUP)
                out[i, rows, 48:64] = r[192 + 32 * end : 224 + 32 * end].reshape(2, 16, GROUP)
        return 0

    looped(project_near, NGROUP, 4)
    for copy in far:
        copy.wait_recv()
    looped(project_far, NGROUP, 4)
    g_copy.wait()

    def query_block(b, hg):
        return block_diagonal(q[hg, pl.ds(64 * b, 64)])

    def grad_block(b, hg):
        lanes = slice(hg * GROUP, (hg + 1) * GROUP) if isinstance(hg, int) else pl.ds(pl.multiple_of(hg * GROUP, GROUP), GROUP)
        return block_diagonal(g[pl.ds(4 * b, 4), :, lanes].reshape(64, GROUP))

    def attend(b, hg):
        keys = k[hg, pl.ds(2 * b, 6)].reshape(384, GROUP)
        vals = v[hg, pl.ds(2 * b, 6)].reshape(384, GROUP)
        masked = bias[b]
        s = dot(keys, query_block(b, hg), NT) + jnp.concatenate([masked, masked], 1)
        e = jnp.exp(s - jnp.max(s, 0, keepdims=True))
        p = e * (1.0 / jnp.sum(e, 0, keepdims=True))
        dp = dot(vals, grad_block(b, hg), NT)
        delta = jnp.sum(p * dp, 0, keepdims=True)
        dscores[b, hg] = (p * (dp - delta)).astype(BF16)
        probs[b, hg] = p.astype(BF16)

    def attend_block(b):
        for hg in range(NGROUP):
            attend(b, hg)

    attend_block(0)
    attend_block(3)

    tensors = ((dscores, query_block), (probs, grad_block))

    def grad_caps(hg, _):
        for index, (weights, block) in enumerate(tensors):
            lanes = pl.ds(pl.multiple_of(index * CHAN + hg * GROUP, GROUP), GROUP)
            for end, b in ((0, 0), (1, 3)):
                r = dot(weights[b, hg, 256 * end : 256 * end + 128], block(b, hg), NN).astype(BF16)
                for dst, src, size in ((0, 0, 32), (32, 64, 32), (64, 32, 16), (80, 96, 16), (96, 48, 16), (112, 112, 16)):
                    grads_cap[128 * end + dst : 128 * end + dst + size, lanes] = r[src : src + size]
        return 0

    looped(grad_caps, NGROUP, 4)

    def back_caps(n, _):
        lanes = pl.ds(pl.multiple_of(n * GROUP, GROUP), GROUP)
        cap_send[:, lanes] = dot(grads_cap[...], w[lanes, CHAN:], NT).astype(BF16)
        return 0

    looped(back_caps, NGROUP, 4)
    back_up = send(cap_send.at[0:128], cap_recv.at[128:256], up)
    back_down = send(cap_send.at[128:256], cap_recv.at[0:128], down)

    attend_block(1)
    attend_block(2)

    def window_sums(weights, block, hg, start, size):
        parts = []
        for b in range(BLOCKS):
            rows = weights[b, hg].reshape(6, 64, GROUP)[:, start : start + size].reshape(6 * size, GROUP)
            parts.append(dot(rows, block(b, hg), NN))
        sums = []
        for p in range(2, 10):
            terms = [parts[b][(p - 2 * b) * size : (p - 2 * b + 1) * size] for b in range(BLOCKS) if 0 <= p - 2 * b < 6]
            sums.append(sum(terms[1:], terms[0]))
        return sums

    def grad_sides(hg, _):
        for index, (weights, block) in enumerate(tensors):
            lanes = pl.ds(pl.multiple_of(index * CHAN + hg * GROUP, GROUP), GROUP)
            sums = window_sums(weights, block, hg, 32, 32)
            for slot, p in enumerate((0, 1, 6, 7, 2, 3, 4, 5)):
                r = sums[p].astype(BF16)
                grads_side[16 * slot : 16 * slot + 16, lanes] = r[:16]
                grads_side[128 + 16 * slot : 144 + 16 * slot, lanes] = r[16:]
        return 0

    looped(grad_sides, NGROUP, 4)

    def back_sides(n, _):
        lanes = pl.ds(pl.multiple_of(n * GROUP, GROUP), GROUP)
        r = dot(grads_side[...], w[lanes, CHAN:], NT)
        for side in range(2):
            side_edge[side, :, lanes] = r[128 * side : 128 * side + 64]
            side_send[side, 64:128, lanes] = r[128 * side + 64 : 128 * side + 128].astype(BF16)
        return 0

    looped(back_sides, NGROUP, 4)
    returns = [
        send(side_send.at[0, 64:128], side_recv.at[1, 64:128], left),
        send(side_send.at[1, 64:128], side_recv.at[0, 64:128], right),
    ]

    def grad_own(hg, _):
        for index, (weights, block) in enumerate(tensors):
            lanes = pl.ds(pl.multiple_of((1 + index) * CHAN + hg * GROUP, GROUP), GROUP)
            for p, r in enumerate(window_sums(weights, block, hg, 0, 32)):
                grads_own[32 * p : 32 * p + 32, lanes] = r.astype(BF16)
        return 0

    looped(grad_own, NGROUP, 4)

    def outputs(b, _):
        rows = pl.ds(64 * b, 64)
        for hg in range(NGROUP):
            lanes = slice(hg * GROUP, (hg + 1) * GROUP)
            keys = k[hg, pl.ds(2 * b, 6)].reshape(384, GROUP)
            vals = v[hg, pl.ds(2 * b, 6)].reshape(384, GROUP)
            att_ref[rows, lanes] = take_diagonal(dot(probs[b, hg], vals, TN)).astype(BF16)
            grads_own[rows, lanes] = (take_diagonal(dot(dscores[b, hg], keys, TN)) * 0.125).astype(BF16)
        return 0

    outputs(0, 0)

    back_up.wait_recv()
    back_down.wait_recv()
    for side in range(2):
        for end in range(2):
            rows = slice(32 * end, 32 * end + 32)
            rim = slice(128 * end + 64 + 32 * side, 128 * end + 96 + 32 * side)
            side_send[side, rows] = (side_edge[side, rows] + cap_recv[rim].astype(F32)).astype(BF16)
    returns.append(send(side_send.at[0, 0:64], side_recv.at[1, 0:64], left))
    returns.append(send(side_send.at[1, 0:64], side_recv.at[0, 0:64], right))

    lax.fori_loop(1, BLOCKS, outputs, 0)
    stores = [fetch(5, att_ref, att_out)]

    def back_own(n, _):
        lanes = pl.ds(pl.multiple_of(n * GROUP, GROUP), GROUP)
        r = dot(grads_own[...], w[lanes, :], NT)
        own_out[0:64, lanes] = r[:64] + cap_recv[0:64, lanes].astype(F32)
        own_out[64:192, lanes] = r[64:192]
        own_out[192:256, lanes] = r[192:] + cap_recv[128:192, lanes].astype(F32)
        return 0

    looped(back_own, NGROUP, 4)

    def finish(slots):
        for slot in slots:
            both = jnp.concatenate([side_recv[side, 8 * slot : 8 * slot + 8].astype(F32) for side in range(2)], 0)
            rows = slice(16 * OUTER_FIRST[slot], 16 * OUTER_FIRST[slot] + 16)
            fg_ref[rows] = (own_out[rows] + both).astype(BF16)

    for copy in returns[:2]:
        copy.wait_recv()
    finish(range(8, 16))
    stores.append(fetch(6, fg_ref.at[64:192], grad_out.at[64:192]))
    for copy in returns[2:]:
        copy.wait_recv()
    finish(range(8))
    stores.append(fetch(7, fg_ref.at[0:64], grad_out.at[0:64]))
    stores.append(fetch(8, fg_ref.at[192:256], grad_out.at[192:256]))
    for copy in stores:
        copy.wait()
    for copy in sent:
        copy.wait_send()


def hand_over(att_ref, grad_ref, att_out, grad_out, held, in_sem, out_sem):
    parts = []
    for index, (src, dst) in enumerate(((att_ref, att_out), (grad_ref, grad_out))):
        for part in range(4):
            rows, slot = slice(64 * part, 64 * part + 64), 4 * index + part
            fetch = pltpu.make_async_copy(src.at[rows], held.at[slot], in_sem.at[slot])
            store = pltpu.make_async_copy(held.at[slot], dst.at[rows], out_sem.at[slot])
            fetch.start()
            parts.append((fetch, store))
    for fetch, store in parts:
        fetch.wait()
        store.start()
    for _, store in parts:
        store.wait()


def shards(features, w_qkv, cotangent, row_reach, col_reach):
    smem = pl.BlockSpec(memory_space=pltpu.SMEM)
    any_space = pl.BlockSpec(memory_space=pl.ANY)
    flat = [jax.ShapeDtypeStruct((256, CHAN), BF16)] * 2
    att, grad = pl.pallas_call(
        kernel,
        out_shape=flat,
        in_specs=[any_space, any_space, any_space, smem, smem],
        out_specs=[any_space, any_space],
        scratch_shapes=[
            pltpu.VMEM((256, CHAN), BF16),
            pltpu.VMEM((512, CHAN), BF16),
            pltpu.VMEM((2, 128, CHAN), BF16),
            pltpu.VMEM((CHAN, 3 * CHAN), BF16),
            pltpu.VMEM((16, 16, CHAN), BF16),
            pltpu.VMEM((NGROUP, 256, GROUP), BF16),
            pltpu.VMEM((NGROUP, 12, 64, GROUP), BF16),
            pltpu.VMEM((NGROUP, 12, 64, GROUP), BF16),
            pltpu.VMEM((BLOCKS, 384, 128), F32),
            pltpu.VMEM((BLOCKS, NGROUP, 384, GROUP), BF16),
            pltpu.VMEM((BLOCKS, NGROUP, 384, GROUP), BF16),
            pltpu.VMEM((256, 2 * CHAN), BF16),
            pltpu.VMEM((256, 2 * CHAN), BF16),
            pltpu.VMEM((256, 3 * CHAN), BF16),
            pltpu.VMEM((2, 64, CHAN), F32),
            pltpu.VMEM((256, CHAN), F32),
            pltpu.VMEM((256, CHAN), BF16),
            pltpu.VMEM((256, CHAN), BF16),
            pltpu.VMEM((2, 128, CHAN), BF16),
            pltpu.VMEM((2, 128, CHAN), BF16),
            pltpu.VMEM((256, CHAN), BF16),
            pltpu.VMEM((256, CHAN), BF16),
            pltpu.SemaphoreType.DMA((9,)),
            pltpu.SemaphoreType.DMA((16,)),
            pltpu.SemaphoreType.DMA((16,)),
        ],
        compiler_params=pltpu.CompilerParams(
            collective_id=0, has_side_effects=True, vmem_limit_bytes=56 << 20
        ),
        name="sphere_attention",
    )(features.reshape(256, CHAN), w_qkv, cotangent, row_reach, col_reach)
    att, grad = pl.pallas_call(
        hand_over,
        out_shape=flat,
        in_specs=[any_space, any_space],
        out_specs=[any_space, any_space],
        scratch_shapes=[
            pltpu.VMEM((8, 64, CHAN), BF16),
            pltpu.SemaphoreType.DMA((8,)),
            pltpu.SemaphoreType.DMA((8,)),
        ],
        name="hand_over",
    )(att, grad)
    return att.reshape(features.shape), grad.reshape(features.shape)


def solution(mesh):
    placed = (P("lat", "lon", None), P(), P("lat", "lon", None), P(), P())
    return jax.shard_map(
        shards,
        mesh=mesh,
        in_specs=placed,
        out_specs=(P("lat", "lon", None), P("lat", "lon", None)),
        check_vma=False,
    )
```

```python
import jax
import jax.numpy as jnp
from jax import lax
from jax.experimental import pallas as pl
from jax.experimental.pallas import tpu as pltpu
from jax.sharding import PartitionSpec as P

HEADS = 16
RMAX = 4
CMAX = 8
CHAN = 1024
GROUP = 256
NGROUP = CHAN // GROUP
BLOCKS = 4
OUTER_FIRST = (0, 1, 2, 3, 12, 13, 14, 15, 4, 5, 6, 7, 8, 9, 10, 11)
F32 = jnp.float32
BF16 = jnp.bfloat16
MESH = pl.DeviceIdType.MESH
NN = (((1,), (0,)), ((), ()))
NT = (((1,), (1,)), ((), ()))
TN = (((0,), (0,)), ((), ()))


def dot(a, b, dims):
    return lax.dot_general(a, b, dims, preferred_element_type=F32)


def block_diagonal(x):
    rows = lax.broadcasted_iota(jnp.int32, (256, GROUP), 0) // 64
    cols = lax.broadcasted_iota(jnp.int32, (256, GROUP), 1) // 64
    return jnp.where(rows == cols, jnp.concatenate([x] * 4, 0), jnp.zeros((), x.dtype))


def take_diagonal(o):
    cols = lax.broadcasted_iota(jnp.int32, (64, GROUP), 1) // 64
    out = o[:64]
    for head in range(1, 4):
        out = jnp.where(cols == head, o[64 * head : 64 * head + 64], out)
    return out


def looped(body, count, unroll):
    def step(i, carry):
        for j in range(unroll):
            body(i * unroll + j, carry)
        return carry

    if unroll == count:
        step(0, 0)
    else:
        lax.fori_loop(0, count // unroll, step, 0)


def kernel(
    x_hbm, w_hbm, g_hbm, rr_ref, cc_ref, att_out, grad_out,
    xm, xh, edges, w, g, q, q_diag, g_diag, k, v, bias, probs, dscores,
    grads_cap, grads_side, grads_own, side_edge, own_out,
    cap_send, cap_recv, side_send, side_recv, att_ref, fg_ref,
    local_sem, send_sem, recv_sem,
):
    lat, lon = lax.axis_index("lat"), lax.axis_index("lon")
    n_lat, n_lon = lax.axis_size("lat"), lax.axis_size("lon")
    up = (lax.rem(lat + n_lat - 1, n_lat), lon)
    down = (lax.rem(lat + 1, n_lat), lon)
    left = (lat, lax.rem(lon + n_lon - 1, n_lon))
    right = (lat, lax.rem(lon + 1, n_lon))

    barrier = pltpu.get_barrier_semaphore()
    for device in (up, down, left, right):
        pl.semaphore_signal(barrier, inc=1, device_id=device, device_id_type=MESH)

    def fetch(index, src, dst):
        copy = pltpu.make_async_copy(src, dst, local_sem.at[index])
        copy.start()
        return copy

    own_copy = fetch(0, x_hbm, xm)
    w_copies = []
    for part in range(3):
        cols = slice(part * CHAN, (part + 1) * CHAN)
        w_copies.append(fetch(1 + part, w_hbm.at[:, cols], w.at[:, cols]))
    g_copy = fetch(4, g_hbm, g)

    own_copy.wait()
    for slot, row in enumerate(OUTER_FIRST):
        edges[0, 8 * slot : 8 * slot + 8] = xm[16 * row : 16 * row + 8]
        edges[1, 8 * slot : 8 * slot + 8] = xm[16 * row + 8 : 16 * row + 16]
    pl.semaphore_wait(barrier, 4)

    sent = []

    def send(src, dst, device):
        index = len(sent)
        copy = pltpu.make_async_remote_copy(
            src_ref=src,
            dst_ref=dst,
            send_sem=send_sem.at[index],
            recv_sem=recv_sem.at[index],
            device_id=device,
            device_id_type=MESH,
        )
        copy.start()
        sent.append(copy)
        return copy

    near = [
        send(edges.at[0, 0:64], xh.at[64:128], left),
        send(edges.at[1, 0:64], xh.at[0:64], right),
        send(xm.at[0:64], xh.at[192:256], up),
        send(xm.at[192:256], xh.at[128:192], down),
    ]
    far = [
        send(edges.at[0, 64:128], xh.at[320:384], left),
        send(edges.at[1, 64:128], xh.at[256:320], right),
    ]

    first_row = lat * 16
    height = n_lat * 16
    lane = lax.broadcasted_iota(jnp.int32, (1, 128), 1)
    q_row, q_col = lane % 64 // 16, lane % 16
    cell = lax.broadcasted_iota(jnp.int32, (384, 1), 0)
    pair, place = cell // 64, cell % 64
    own = place < 32
    k_row = 2 * pair + jnp.where(own, place // 16, place % 16 // 8)
    k_col = jnp.where(own, place % 16, place % 8 + jnp.where(place < 48, -8, 16))
    row_gap = jnp.abs(k_row - RMAX - q_row)
    col_gap = jnp.abs(k_col - q_col)
    for b in range(BLOCKS):
        reach_r = jnp.zeros((1, 128), jnp.int32)
        reach_c = jnp.zeros((1, 128), jnp.int32)
        for row in range(4):
            reach_r = jnp.where(q_row == row, rr_ref[first_row + 4 * b + row], reach_r)
            reach_c = jnp.where(q_row == row, cc_ref[first_row + 4 * b + row], reach_c)
        key_row = first_row + 4 * b - RMAX + k_row
        ok = (row_gap <= reach_r) & (col_gap <= reach_c) & ((key_row >= 0) & (key_row < height))
        bias[b] = jnp.where(ok, 0.0, -1e30)

    def w_cols(part, i):
        return w[:, pl.ds(pl.multiple_of(part * CHAN + i * GROUP, GROUP), GROUP)]

    def project_query(i, _):
        r = dot(xm[...], w_cols(0, i), NN)
        q[i] = r.astype(BF16) * BF16(0.125)
        return 0

    def project_own(part, out):
        def project(i, _):
            r = dot(xm[...], w_cols(part, i), NN).astype(BF16)
            out[i, 2:10, 0:32] = r.reshape(8, 32, GROUP)
            return 0

        looped(project, NGROUP, 4)

    w_copies[0].wait()
    looped(project_query, NGROUP, 4)
    w_copies[1].wait()
    project_own(1, k)
    for copy in near:
        copy.wait_recv()
    for side in range(2):
        rows = 64 * side
        far.append(send(xh.at[rows : rows + 32], xh.at[416 + rows : 448 + rows], up))
        far.append(send(xh.at[rows + 32 : rows + 64], xh.at[384 + rows : 416 + rows], down))
    w_copies[2].wait()
    project_own(2, v)

    def project_near(i, _):
        for part, out in ((1, k), (2, v)):
            r = dot(xh[0:256], w_cols(part, i), NN).astype(BF16)
            for end, rows in ((0, slice(2, 4)), (1, slice(8, 10))):
                out[i, rows, 32:48] = r[32 * end : 32 * end + 32].reshape(2, 16, GROUP)
                out[i, rows, 48:64] = r[64 + 32 * end : 96 + 32 * end].reshape(2, 16, GROUP)
            out[i, 0:2, 0:32] = r[128:192].reshape(2, 32, GROUP)
            out[i, 10:12, 0:32] = r[192:256].reshape(2, 32, GROUP)
        return 0

    def project_far(i, _):
        for part, out in ((1, k), (2, v)):
            r = dot(xh[256:512], w_cols(part, i), NN).astype(BF16)
            out[i, 4:8, 32:48] = r[0:64].reshape(4, 16, GROUP)
            out[i, 4:8, 48:64] = r[64:128].reshape(4, 16, GROUP)
            for end, rows in ((0, slice(0, 2)), (1, slice(10, 12))):
                out[i, rows, 32:48] = r[128 + 32 * end : 160 + 32 * end].reshape(2, 16, GROUP)
                out[i, rows, 48:64] = r[192 + 32 * end : 224 + 32 * end].reshape(2, 16, GROUP)
        return 0

    looped(project_near, NGROUP, 4)
    g_copy.wait()

    def lay_blocks(b, _):
        for hg in range(NGROUP):
            lanes = slice(hg * GROUP, (hg + 1) * GROUP)
            q_diag[b, hg] = block_diagonal(q[hg, pl.ds(64 * b, 64)])
            g_diag[b, hg] = block_diagonal(g[pl.ds(4 * b, 4), :, lanes].reshape(64, GROUP))
        return 0

    lax.fori_loop(0, BLOCKS, lay_blocks, 0)
    for copy in far:
        copy.wait_recv()
    looped(project_far, NGROUP, 4)
    def query_block(b, hg):
        return q_diag[b, hg]

    def grad_block(b, hg):
        return g_diag[b, hg]

    def attend(b, hg):
        keys = k[hg, pl.ds(2 * b, 6)].reshape(384, GROUP)
        vals = v[hg, pl.ds(2 * b, 6)].reshape(384, GROUP)
        masked = bias[b]
        s = dot(keys, query_block(b, hg), NT) + jnp.concatenate([masked, masked], 1)
        e = jnp.exp(s - jnp.max(s, 0, keepdims=True))
        p = e * (1.0 / jnp.sum(e, 0, keepdims=True))
        dp = dot(vals, grad_block(b, hg), NT)
        delta = jnp.sum(p * dp, 0, keepdims=True)
        dscores[b, hg] = (p * (dp - delta)).astype(BF16)
        probs[b, hg] = p.astype(BF16)

    def attend_block(b):
        for hg in range(NGROUP):
            attend(b, hg)

    attend_block(0)
    attend_block(3)

    tensors = ((dscores, query_block), (probs, grad_block))

    def grad_caps(hg, _):
        for index, (weights, block) in enumerate(tensors):
            lanes = pl.ds(pl.multiple_of(index * CHAN + hg * GROUP, GROUP), GROUP)
            for end, b in ((0, 0), (1, 3)):
                r = dot(weights[b, hg, 256 * end : 256 * end + 128], block(b, hg), NN).astype(BF16)
                for dst, src, size in ((0, 0, 32), (32, 64, 32), (64, 32, 16), (80, 96, 16), (96, 48, 16), (112, 112, 16)):
                    grads_cap[128 * end + dst : 128 * end + dst + size, lanes] = r[src : src + size]
        return 0

    looped(grad_caps, NGROUP, 4)

    def back_caps(n, _):
        lanes = pl.ds(pl.multiple_of(n * GROUP, GROUP), GROUP)
        cap_send[:, lanes] = dot(grads_cap[...], w[lanes, CHAN:], NT).astype(BF16)
        return 0

    looped(back_caps, NGROUP, 4)
    back_up = send(cap_send.at[0:128], cap_recv.at[128:256], up)
    back_down = send(cap_send.at[128:256], cap_recv.at[0:128], down)

    attend_block(1)
    attend_block(2)

    def window_sums(weights, block, hg, start, size):
        parts = []
        for b in range(BLOCKS):
            rows = weights[b, hg].reshape(6, 64, GROUP)[:, start : start + size].reshape(6 * size, GROUP)
            parts.append(dot(rows, block(b, hg), NN))
        sums = []
        for p in range(2, 10):
            terms = [parts[b][(p - 2 * b) * size : (p - 2 * b + 1) * size] for b in range(BLOCKS) if 0 <= p - 2 * b < 6]
            sums.append(sum(terms[1:], terms[0]))
        return sums

    def grad_sides(hg, _):
        for index, (weights, block) in enumerate(tensors):
            lanes = pl.ds(pl.multiple_of(index * CHAN + hg * GROUP, GROUP), GROUP)
            sums = window_sums(weights, block, hg, 32, 32)
            for slot, p in enumerate((0, 1, 6, 7, 2, 3, 4, 5)):
                r = sums[p].astype(BF16)
                grads_side[16 * slot : 16 * slot + 16, lanes] = r[:16]
                grads_side[128 + 16 * slot : 144 + 16 * slot, lanes] = r[16:]
        return 0

    looped(grad_sides, NGROUP, 4)

    def back_sides(n, _):
        lanes = pl.ds(pl.multiple_of(n * GROUP, GROUP), GROUP)
        r = dot(grads_side[...], w[lanes, CHAN:], NT)
        for side in range(2):
            side_edge[side, :, lanes] = r[128 * side : 128 * side + 64]
            side_send[side, 64:128, lanes] = r[128 * side + 64 : 128 * side + 128].astype(BF16)
        return 0

    looped(back_sides, NGROUP, 4)
    returns = [
        send(side_send.at[0, 64:128], side_recv.at[1, 64:128], left),
        send(side_send.at[1, 64:128], side_recv.at[0, 64:128], right),
    ]

    def grad_own(hg, _):
        for index, (weights, block) in enumerate(tensors):
            lanes = pl.ds(pl.multiple_of((1 + index) * CHAN + hg * GROUP, GROUP), GROUP)
            for p, r in enumerate(window_sums(weights, block, hg, 0, 32)):
                grads_own[32 * p : 32 * p + 32, lanes] = r.astype(BF16)
        return 0

    looped(grad_own, NGROUP, 4)

    def outputs(b, _):
        rows = pl.ds(64 * b, 64)
        for hg in range(NGROUP):
            lanes = slice(hg * GROUP, (hg + 1) * GROUP)
            keys = k[hg, pl.ds(2 * b, 6)].reshape(384, GROUP)
            vals = v[hg, pl.ds(2 * b, 6)].reshape(384, GROUP)
            att_ref[rows, lanes] = take_diagonal(dot(probs[b, hg], vals, TN)).astype(BF16)
            grads_own[rows, lanes] = (take_diagonal(dot(dscores[b, hg], keys, TN)) * 0.125).astype(BF16)
        return 0


    back_up.wait_recv()
    back_down.wait_recv()
    for side in range(2):
        for end in range(2):
            rows = slice(32 * end, 32 * end + 32)
            rim = slice(128 * end + 64 + 32 * side, 128 * end + 96 + 32 * side)
            side_send[side, rows] = (side_edge[side, rows] + cap_recv[rim].astype(F32)).astype(BF16)
    returns.append(send(side_send.at[0, 0:64], side_recv.at[1, 0:64], left))
    returns.append(send(side_send.at[1, 0:64], side_recv.at[0, 0:64], right))

    lax.fori_loop(0, BLOCKS, outputs, 0)
    stores = [fetch(5, att_ref, att_out)]

    def back_own(n, _):
        lanes = pl.ds(pl.multiple_of(n * GROUP, GROUP), GROUP)
        r = dot(grads_own[...], w[lanes, :], NT)
        own_out[0:64, lanes] = r[:64] + cap_recv[0:64, lanes].astype(F32)
        own_out[64:192, lanes] = r[64:192]
        own_out[192:256, lanes] = r[192:] + cap_recv[128:192, lanes].astype(F32)
        return 0

    looped(back_own, NGROUP, 4)

    def finish(slots):
        for slot in slots:
            both = jnp.concatenate([side_recv[side, 8 * slot : 8 * slot + 8].astype(F32) for side in range(2)], 0)
            rows = slice(16 * OUTER_FIRST[slot], 16 * OUTER_FIRST[slot] + 16)
            fg_ref[rows] = (own_out[rows] + both).astype(BF16)

    for copy in returns[:2]:
        copy.wait_recv()
    finish(range(8, 16))
    stores.append(fetch(6, fg_ref.at[64:192], grad_out.at[64:192]))
    for copy in returns[2:]:
        copy.wait_recv()
    finish(range(8))
    stores.append(fetch(7, fg_ref.at[0:64], grad_out.at[0:64]))
    stores.append(fetch(8, fg_ref.at[192:256], grad_out.at[192:256]))
    for copy in stores:
        copy.wait()
    for copy in sent:
        copy.wait_send()


def hand_over(att_ref, grad_ref, att_out, grad_out, held, in_sem, out_sem):
    parts = []
    for index, (src, dst) in enumerate(((att_ref, att_out), (grad_ref, grad_out))):
        for part in range(4):
            rows, slot = slice(64 * part, 64 * part + 64), 4 * index + part
            fetch = pltpu.make_async_copy(src.at[rows], held.at[slot], in_sem.at[slot])
            store = pltpu.make_async_copy(held.at[slot], dst.at[rows], out_sem.at[slot])
            fetch.start()
            parts.append((fetch, store))
    for fetch, store in parts:
        fetch.wait()
        store.start()
    for _, store in parts:
        store.wait()


def shards(features, w_qkv, cotangent, row_reach, col_reach):
    smem = pl.BlockSpec(memory_space=pltpu.SMEM)
    any_space = pl.BlockSpec(memory_space=pl.ANY)
    flat = [jax.ShapeDtypeStruct((256, CHAN), BF16)] * 2
    att, grad = pl.pallas_call(
        kernel,
        out_shape=flat,
        in_specs=[any_space, any_space, any_space, smem, smem],
        out_specs=[any_space, any_space],
        scratch_shapes=[
            pltpu.VMEM((256, CHAN), BF16),
            pltpu.VMEM((512, CHAN), BF16),
            pltpu.VMEM((2, 128, CHAN), BF16),
            pltpu.VMEM((CHAN, 3 * CHAN), BF16),
            pltpu.VMEM((16, 16, CHAN), BF16),
            pltpu.VMEM((NGROUP, 256, GROUP), BF16),
            pltpu.VMEM((BLOCKS, NGROUP, 256, GROUP), BF16),
            pltpu.VMEM((BLOCKS, NGROUP, 256, GROUP), BF16),
            pltpu.VMEM((NGROUP, 12, 64, GROUP), BF16),
            pltpu.VMEM((NGROUP, 12, 64, GROUP), BF16),
            pltpu.VMEM((BLOCKS, 384, 128), F32),
            pltpu.VMEM((BLOCKS, NGROUP, 384, GROUP), BF16),
            pltpu.VMEM((BLOCKS, NGROUP, 384, GROUP), BF16),
            pltpu.VMEM((256, 2 * CHAN), BF16),
            pltpu.VMEM((256, 2 * CHAN), BF16),
            pltpu.VMEM((256, 3 * CHAN), BF16),
            pltpu.VMEM((2, 64, CHAN), F32),
            pltpu.VMEM((256, CHAN), F32),
            pltpu.VMEM((256, CHAN), BF16),
            pltpu.VMEM((256, CHAN), BF16),
            pltpu.VMEM((2, 128, CHAN), BF16),
            pltpu.VMEM((2, 128, CHAN), BF16),
            pltpu.VMEM((256, CHAN), BF16),
            pltpu.VMEM((256, CHAN), BF16),
            pltpu.SemaphoreType.DMA((9,)),
            pltpu.SemaphoreType.DMA((16,)),
            pltpu.SemaphoreType.DMA((16,)),
        ],
        compiler_params=pltpu.CompilerParams(
            collective_id=0, has_side_effects=True, vmem_limit_bytes=56 << 20
        ),
        name="sphere_attention",
    )(features.reshape(256, CHAN), w_qkv, cotangent, row_reach, col_reach)
    att, grad = pl.pallas_call(
        hand_over,
        out_shape=flat,
        in_specs=[any_space, any_space],
        out_specs=[any_space, any_space],
        scratch_shapes=[
            pltpu.VMEM((8, 64, CHAN), BF16),
            pltpu.SemaphoreType.DMA((8,)),
            pltpu.SemaphoreType.DMA((8,)),
        ],
        name="hand_over",
    )(att, grad)
    return att.reshape(features.shape), grad.reshape(features.shape)


def solution(mesh):
    placed = (P("lat", "lon", None), P(), P("lat", "lon", None), P(), P())
    return jax.shard_map(
        shards,
        mesh=mesh,
        in_specs=placed,
        out_specs=(P("lat", "lon", None), P("lat", "lon", None)),
        check_vma=False,
    )
```

```python
import jax
import jax.numpy as jnp
from jax import lax
from jax.experimental import pallas as pl
from jax.experimental.pallas import tpu as pltpu
from jax.sharding import PartitionSpec as P

HEADS = 16
RMAX = 4
CMAX = 8
CHAN = 1024
GROUP = 256
NGROUP = CHAN // GROUP
BLOCKS = 4
OUTER_FIRST = (0, 1, 2, 3, 12, 13, 14, 15, 4, 5, 6, 7, 8, 9, 10, 11)
F32 = jnp.float32
BF16 = jnp.bfloat16
MESH = pl.DeviceIdType.MESH
NN = (((1,), (0,)), ((), ()))
NT = (((1,), (1,)), ((), ()))
TN = (((0,), (0,)), ((), ()))


def dot(a, b, dims):
    return lax.dot_general(a, b, dims, preferred_element_type=F32)


def block_diagonal(x):
    rows = lax.broadcasted_iota(jnp.int32, (256, GROUP), 0) // 64
    cols = lax.broadcasted_iota(jnp.int32, (256, GROUP), 1) // 64
    return jnp.where(rows == cols, jnp.concatenate([x] * 4, 0), jnp.zeros((), x.dtype))


def take_diagonal(o):
    cols = lax.broadcasted_iota(jnp.int32, (64, GROUP), 1) // 64
    out = o[:64]
    for head in range(1, 4):
        out = jnp.where(cols == head, o[64 * head : 64 * head + 64], out)
    return out


def looped(body, count, unroll):
    def step(i, carry):
        for j in range(unroll):
            body(i * unroll + j, carry)
        return carry

    if unroll == count:
        step(0, 0)
    else:
        lax.fori_loop(0, count // unroll, step, 0)


def kernel(
    x_hbm, w_hbm, g_hbm, rr_ref, cc_ref, att_out, grad_out,
    xm, xh, edges, w, g, q, q_diag, g_diag, k, v, bias, probs, dscores,
    grads_cap, grads_side, grads_own, side_edge, own_out,
    cap_send, cap_recv, side_send, side_recv, att_ref, fg_ref,
    local_sem, send_sem, recv_sem,
):
    lat, lon = lax.axis_index("lat"), lax.axis_index("lon")
    n_lat, n_lon = lax.axis_size("lat"), lax.axis_size("lon")
    up = (lax.rem(lat + n_lat - 1, n_lat), lon)
    down = (lax.rem(lat + 1, n_lat), lon)
    left = (lat, lax.rem(lon + n_lon - 1, n_lon))
    right = (lat, lax.rem(lon + 1, n_lon))

    barrier = pltpu.get_barrier_semaphore()
    for device in (up, down, left, right):
        pl.semaphore_signal(barrier, inc=1, device_id=device, device_id_type=MESH)

    def fetch(index, src, dst):
        copy = pltpu.make_async_copy(src, dst, local_sem.at[index])
        copy.start()
        return copy

    own_copy = fetch(0, x_hbm, xm)
    w_copies = []
    for part in range(3):
        cols = slice(part * CHAN, (part + 1) * CHAN)
        w_copies.append(fetch(1 + part, w_hbm.at[:, cols], w.at[:, cols]))
    g_copy = fetch(4, g_hbm, g)

    own_copy.wait()
    for slot, row in enumerate(OUTER_FIRST):
        edges[0, 8 * slot : 8 * slot + 8] = xm[16 * row : 16 * row + 8]
        edges[1, 8 * slot : 8 * slot + 8] = xm[16 * row + 8 : 16 * row + 16]
    pl.semaphore_wait(barrier, 4)

    sent = []

    def send(src, dst, device):
        index = len(sent)
        copy = pltpu.make_async_remote_copy(
            src_ref=src,
            dst_ref=dst,
            send_sem=send_sem.at[index],
            recv_sem=recv_sem.at[index],
            device_id=device,
            device_id_type=MESH,
        )
        copy.start()
        sent.append(copy)
        return copy

    near = [
        send(edges.at[0, 0:64], xh.at[64:128], left),
        send(edges.at[1, 0:64], xh.at[0:64], right),
        send(xm.at[0:64], xh.at[192:256], up),
        send(xm.at[192:256], xh.at[128:192], down),
    ]
    far = [
        send(edges.at[0, 64:128], xh.at[320:384], left),
        send(edges.at[1, 64:128], xh.at[256:320], right),
    ]

    first_row = lat * 16
    height = n_lat * 16
    lane = lax.broadcasted_iota(jnp.int32, (1, 128), 1)
    q_row, q_col = lane % 64 // 16, lane % 16
    cell = lax.broadcasted_iota(jnp.int32, (384, 1), 0)
    pair, place = cell // 64, cell % 64
    own = place < 32
    k_row = 2 * pair + jnp.where(own, place // 16, place % 16 // 8)
    k_col = jnp.where(own, place % 16, place % 8 + jnp.where(place < 48, -8, 16))
    row_gap = jnp.abs(k_row - RMAX - q_row)
    col_gap = jnp.abs(k_col - q_col)
    for b in range(BLOCKS):
        reach_r = jnp.zeros((1, 128), jnp.int32)
        reach_c = jnp.zeros((1, 128), jnp.int32)
        for row in range(4):
            reach_r = jnp.where(q_row == row, rr_ref[first_row + 4 * b + row], reach_r)
            reach_c = jnp.where(q_row == row, cc_ref[first_row + 4 * b + row], reach_c)
        key_row = first_row + 4 * b - RMAX + k_row
        ok = (row_gap <= reach_r) & (col_gap <= reach_c) & ((key_row >= 0) & (key_row < height))
        bias[b] = jnp.where(ok, 0.0, -1e30)

    def w_cols(part, i):
        return w[:, pl.ds(pl.multiple_of(part * CHAN + i * GROUP, GROUP), GROUP)]

    def project_query(i, _):
        r = dot(xm[...], w_cols(0, i), NN)
        q[i] = r.astype(BF16) * BF16(0.125)
        return 0

    def project_own(part, out):
        def project(i, _):
            r = dot(xm[...], w_cols(part, i), NN).astype(BF16)
            out[i, 2:10, 0:32] = r.reshape(8, 32, GROUP)
            return 0

        looped(project, NGROUP, 4)

    w_copies[0].wait()
    looped(project_query, NGROUP, 4)
    w_copies[1].wait()
    project_own(1, k)
    for copy in near:
        copy.wait_recv()
    for side in range(2):
        rows = 64 * side
        far.append(send(xh.at[rows : rows + 32], xh.at[416 + rows : 448 + rows], up))
        far.append(send(xh.at[rows + 32 : rows + 64], xh.at[384 + rows : 416 + rows], down))
    w_copies[2].wait()
    project_own(2, v)

    def project_near(i, _):
        for part, out in ((1, k), (2, v)):
            r = dot(xh[0:256], w_cols(part, i), NN).astype(BF16)
            for end, rows in ((0, slice(2, 4)), (1, slice(8, 10))):
                out[i, rows, 32:48] = r[32 * end : 32 * end + 32].reshape(2, 16, GROUP)
                out[i, rows, 48:64] = r[64 + 32 * end : 96 + 32 * end].reshape(2, 16, GROUP)
            out[i, 0:2, 0:32] = r[128:192].reshape(2, 32, GROUP)
            out[i, 10:12, 0:32] = r[192:256].reshape(2, 32, GROUP)
        return 0

    def project_far(i, _):
        for part, out in ((1, k), (2, v)):
            r = dot(xh[256:512], w_cols(part, i), NN).astype(BF16)
            out[i, 4:8, 32:48] = r[0:64].reshape(4, 16, GROUP)
            out[i, 4:8, 48:64] = r[64:128].reshape(4, 16, GROUP)
            for end, rows in ((0, slice(0, 2)), (1, slice(10, 12))):
                out[i, rows, 32:48] = r[128 + 32 * end : 160 + 32 * end].reshape(2, 16, GROUP)
                out[i, rows, 48:64] = r[192 + 32 * end : 224 + 32 * end].reshape(2, 16, GROUP)
        return 0

    looped(project_near, NGROUP, 4)
    g_copy.wait()

    def lay_blocks(b, _):
        for hg in range(NGROUP):
            lanes = slice(hg * GROUP, (hg + 1) * GROUP)
            q_diag[b, hg] = block_diagonal(q[hg, pl.ds(64 * b, 64)])
            g_diag[b, hg] = block_diagonal(g[pl.ds(4 * b, 4), :, lanes].reshape(64, GROUP))
        return 0

    lax.fori_loop(0, BLOCKS, lay_blocks, 0)
    for copy in far:
        copy.wait_recv()
    looped(project_far, NGROUP, 4)
    def query_block(b, hg):
        return q_diag[b, hg]

    def grad_block(b, hg):
        return g_diag[b, hg]

    def attend(b, hg):
        keys = k[hg, pl.ds(2 * b, 6)].reshape(384, GROUP)
        vals = v[hg, pl.ds(2 * b, 6)].reshape(384, GROUP)
        masked = bias[b]
        s = dot(keys, query_block(b, hg), NT) + jnp.concatenate([masked, masked], 1)
        e = jnp.exp(s - jnp.max(s, 0, keepdims=True))
        p = e * (1.0 / jnp.sum(e, 0, keepdims=True))
        dp = dot(vals, grad_block(b, hg), NT)
        delta = jnp.sum(p * dp, 0, keepdims=True)
        dscores[b, hg] = (p * (dp - delta)).astype(BF16)
        probs[b, hg] = p.astype(BF16)

    def attend_block(b):
        for hg in range(NGROUP):
            attend(b, hg)

    attend_block(0)
    attend_block(3)

    tensors = ((dscores, query_block), (probs, grad_block))

    def grad_caps(hg, _):
        for index, (weights, block) in enumerate(tensors):
            lanes = pl.ds(pl.multiple_of(index * CHAN + hg * GROUP, GROUP), GROUP)
            for end, b in ((0, 0), (1, 3)):
                r = dot(weights[b, hg, 256 * end : 256 * end + 128], block(b, hg), NN).astype(BF16)
                for dst, src, size in ((0, 0, 32), (32, 64, 32), (64, 32, 16), (80, 96, 16), (96, 48, 16), (112, 112, 16)):
                    grads_cap[128 * end + dst : 128 * end + dst + size, lanes] = r[src : src + size]
        return 0

    looped(grad_caps, NGROUP, 4)

    def back_caps(n, _):
        lanes = pl.ds(pl.multiple_of(n * GROUP, GROUP), GROUP)
        cap_send[:, lanes] = dot(grads_cap[...], w[lanes, CHAN:], NT).astype(BF16)
        return 0

    looped(back_caps, NGROUP, 4)
    back_up = send(cap_send.at[0:128], cap_recv.at[128:256], up)
    back_down = send(cap_send.at[128:256], cap_recv.at[0:128], down)

    attend_block(1)
    attend_block(2)

    def window_sums(weights, block, hg, start, size):
        sums = [None] * 8
        for b in range(BLOCKS):
            first, last = max(2 - 2 * b, 0), min(10 - 2 * b, 6)
            rows = weights[b, hg].reshape(6, 64, GROUP)[first:last, start : start + size]
            r = dot(rows.reshape((last - first) * size, GROUP), block(b, hg), NN)
            for p in range(first, last):
                term = r[(p - first) * size : (p - first + 1) * size]
                slot = p + 2 * b - 2
                sums[slot] = term if sums[slot] is None else sums[slot] + term
        return sums

    def grad_sides(hg, _):
        for index, (weights, block) in enumerate(tensors):
            lanes = pl.ds(pl.multiple_of(index * CHAN + hg * GROUP, GROUP), GROUP)
            sums = window_sums(weights, block, hg, 32, 32)
            for slot, p in enumerate((0, 1, 6, 7, 2, 3, 4, 5)):
                r = sums[p].astype(BF16)
                grads_side[16 * slot : 16 * slot + 16, lanes] = r[:16]
                grads_side[128 + 16 * slot : 144 + 16 * slot, lanes] = r[16:]
        return 0

    looped(grad_sides, NGROUP, 4)

    def back_sides(n, _):
        lanes = pl.ds(pl.multiple_of(n * GROUP, GROUP), GROUP)
        r = dot(grads_side[...], w[lanes, CHAN:], NT)
        for side in range(2):
            side_edge[side, :, lanes] = r[128 * side : 128 * side + 64]
            side_send[side, 64:128, lanes] = r[128 * side + 64 : 128 * side + 128].astype(BF16)
        return 0

    looped(back_sides, NGROUP, 4)
    returns = [
        send(side_send.at[0, 64:128], side_recv.at[1, 64:128], left),
        send(side_send.at[1, 64:128], side_recv.at[0, 64:128], right),
    ]

    def grad_own(hg, _):
        for index, (weights, block) in enumerate(tensors):
            lanes = pl.ds(pl.multiple_of((1 + index) * CHAN + hg * GROUP, GROUP), GROUP)
            for p, r in enumerate(window_sums(weights, block, hg, 0, 32)):
                grads_own[32 * p : 32 * p + 32, lanes] = r.astype(BF16)
        return 0

    looped(grad_own, NGROUP, 4)

    def outputs(b, _):
        rows = pl.ds(64 * b, 64)
        for hg in range(NGROUP):
            lanes = slice(hg * GROUP, (hg + 1) * GROUP)
            keys = k[hg, pl.ds(2 * b, 6)].reshape(384, GROUP)
            vals = v[hg, pl.ds(2 * b, 6)].reshape(384, GROUP)
            att_ref[rows, lanes] = take_diagonal(dot(probs[b, hg], vals, TN)).astype(BF16)
            grads_own[rows, lanes] = (take_diagonal(dot(dscores[b, hg], keys, TN)) * 0.125).astype(BF16)
        return 0


    back_up.wait_recv()
    back_down.wait_recv()
    for side in range(2):
        for end in range(2):
            rows = slice(32 * end, 32 * end + 32)
            rim = slice(128 * end + 64 + 32 * side, 128 * end + 96 + 32 * side)
            side_send[side, rows] = (side_edge[side, rows] + cap_recv[rim].astype(F32)).astype(BF16)
    returns.append(send(side_send.at[0, 0:64], side_recv.at[1, 0:64], left))
    returns.append(send(side_send.at[1, 0:64], side_recv.at[0, 0:64], right))

    lax.fori_loop(0, BLOCKS, outputs, 0)
    stores = [fetch(5, att_ref, att_out)]

    def back_own(n, _):
        lanes = pl.ds(pl.multiple_of(n * GROUP, GROUP), GROUP)
        r = dot(grads_own[...], w[lanes, :], NT)
        own_out[0:64, lanes] = r[:64] + cap_recv[0:64, lanes].astype(F32)
        own_out[64:192, lanes] = r[64:192]
        own_out[192:256, lanes] = r[192:] + cap_recv[128:192, lanes].astype(F32)
        return 0

    looped(back_own, NGROUP, 4)

    def finish(slots):
        for slot in slots:
            both = jnp.concatenate([side_recv[side, 8 * slot : 8 * slot + 8].astype(F32) for side in range(2)], 0)
            rows = slice(16 * OUTER_FIRST[slot], 16 * OUTER_FIRST[slot] + 16)
            fg_ref[rows] = (own_out[rows] + both).astype(BF16)

    for copy in returns[:2]:
        copy.wait_recv()
    finish(range(8, 16))
    stores.append(fetch(6, fg_ref.at[64:192], grad_out.at[64:192]))
    for copy in returns[2:]:
        copy.wait_recv()
    finish(range(8))
    stores.append(fetch(7, fg_ref.at[0:64], grad_out.at[0:64]))
    stores.append(fetch(8, fg_ref.at[192:256], grad_out.at[192:256]))
    for copy in stores:
        copy.wait()
    for copy in sent:
        copy.wait_send()


def hand_over(att_ref, grad_ref, att_out, grad_out, held, in_sem, out_sem):
    parts = []
    for index, (src, dst) in enumerate(((att_ref, att_out), (grad_ref, grad_out))):
        for part in range(4):
            rows, slot = slice(64 * part, 64 * part + 64), 4 * index + part
            fetch = pltpu.make_async_copy(src.at[rows], held.at[slot], in_sem.at[slot])
            store = pltpu.make_async_copy(held.at[slot], dst.at[rows], out_sem.at[slot])
            fetch.start()
            parts.append((fetch, store))
    for fetch, store in parts:
        fetch.wait()
        store.start()
    for _, store in parts:
        store.wait()


def shards(features, w_qkv, cotangent, row_reach, col_reach):
    smem = pl.BlockSpec(memory_space=pltpu.SMEM)
    any_space = pl.BlockSpec(memory_space=pl.ANY)
    flat = [jax.ShapeDtypeStruct((256, CHAN), BF16)] * 2
    att, grad = pl.pallas_call(
        kernel,
        out_shape=flat,
        in_specs=[any_space, any_space, any_space, smem, smem],
        out_specs=[any_space, any_space],
        scratch_shapes=[
            pltpu.VMEM((256, CHAN), BF16),
            pltpu.VMEM((512, CHAN), BF16),
            pltpu.VMEM((2, 128, CHAN), BF16),
            pltpu.VMEM((CHAN, 3 * CHAN), BF16),
            pltpu.VMEM((16, 16, CHAN), BF16),
            pltpu.VMEM((NGROUP, 256, GROUP), BF16),
            pltpu.VMEM((BLOCKS, NGROUP, 256, GROUP), BF16),
            pltpu.VMEM((BLOCKS, NGROUP, 256, GROUP), BF16),
            pltpu.VMEM((NGROUP, 12, 64, GROUP), BF16),
            pltpu.VMEM((NGROUP, 12, 64, GROUP), BF16),
            pltpu.VMEM((BLOCKS, 384, 128), F32),
            pltpu.VMEM((BLOCKS, NGROUP, 384, GROUP), BF16),
            pltpu.VMEM((BLOCKS, NGROUP, 384, GROUP), BF16),
            pltpu.VMEM((256, 2 * CHAN), BF16),
            pltpu.VMEM((256, 2 * CHAN), BF16),
            pltpu.VMEM((256, 3 * CHAN), BF16),
            pltpu.VMEM((2, 64, CHAN), F32),
            pltpu.VMEM((256, CHAN), F32),
            pltpu.VMEM((256, CHAN), BF16),
            pltpu.VMEM((256, CHAN), BF16),
            pltpu.VMEM((2, 128, CHAN), BF16),
            pltpu.VMEM((2, 128, CHAN), BF16),
            pltpu.VMEM((256, CHAN), BF16),
            pltpu.VMEM((256, CHAN), BF16),
            pltpu.SemaphoreType.DMA((9,)),
            pltpu.SemaphoreType.DMA((16,)),
            pltpu.SemaphoreType.DMA((16,)),
        ],
        compiler_params=pltpu.CompilerParams(
            collective_id=0, has_side_effects=True, vmem_limit_bytes=56 << 20
        ),
        name="sphere_attention",
    )(features.reshape(256, CHAN), w_qkv, cotangent, row_reach, col_reach)
    att, grad = pl.pallas_call(
        hand_over,
        out_shape=flat,
        in_specs=[any_space, any_space],
        out_specs=[any_space, any_space],
        scratch_shapes=[
            pltpu.VMEM((8, 64, CHAN), BF16),
            pltpu.SemaphoreType.DMA((8,)),
            pltpu.SemaphoreType.DMA((8,)),
        ],
        name="hand_over",
    )(att, grad)
    return att.reshape(features.shape), grad.reshape(features.shape)


def solution(mesh):
    placed = (P("lat", "lon", None), P(), P("lat", "lon", None), P(), P())
    return jax.shard_map(
        shards,
        mesh=mesh,
        in_specs=placed,
        out_specs=(P("lat", "lon", None), P("lat", "lon", None)),
        check_vma=False,
    )
```
